32 devices in a mesh: expert: 4 (over x, core), tensor: 8 (over z, y).
Axes of the slice: x: 2, y: 2, z: 4, core: 2. Of those that a mesh axis runs over, the one named last changes fastest.
Arguments:
- tokens: bfloat16 [192, 6144], P('tensor'), may hold values from -6 to 6
- expert_ids: int32 [192, 2], P('tensor'), may hold values from 0 to 3, all different within a row; in each aligned block of 24 rows (0 to 23, 24 to 47, ...) at most 24 rows name the same one
- gate_units: int32 [192, 2], P('tensor'), may hold values from 1 to 65535
- gate_weight: bfloat16 [4, 6144, 8192], P('expert', None, 'tensor'), may hold values from -0.078125 to 0.078125
- up_weight: bfloat16 [4, 6144, 8192], P('expert', None, 'tensor'), may hold values from -0.078125 to 0.078125
- down_weight: bfloat16 [4, 6144, 8192], P('expert', 'tensor'), may hold values from -0.0625 to 0.0625
Outputs:
- expert_mix: bfloat16 [192, 6144], P('tensor', 'expert')
The draws below stay inside these ranges and needn't reach their ends.
Inputs may be any that keep to these rules, and one draw needn't show every extreme that they name: `expert_ids`: within each aligned block of 24 rows (the tokens of one tensor index) the two ids of a row differ and no expert is named by more than 24 rows; in every draw some expert is named by exactly 24 rows of some block, and every expert is named somewhere.
All inputs are finite; a program needn't handle non-finite values.
Results may differ from the reference program's by a relative error of at most 0.0057.
Values may be sent and summed in bfloat16 or wider, within the bound.
No kernel may reach another device: no remote copies, remote signals or barrier semaphores. Data moves between devices by JAX's collectives and lax.ppermute only.
A program may use at most 128 MiB of HBM per device.

```python
import math
import jax
import jax.numpy as jnp
import numpy as np
from jax import lax

D = 6144
FF = 8192
TOPK = 2
TOK_T = 24
EXPERTS = 4
CAPT = 24
TOKENS = 192
N_TENSOR = 8


def set_ends(result, own_key, smallest, top_value):
    shape = result.shape
    place = [jax.random.randint(jax.random.fold_in(own_key, axis), (), 0, shape[axis]) for axis in range(len(shape))]
    result = result.at[tuple(place)].set(smallest)
    longest = shape.index(max(shape))
    place[longest] = (place[longest] + 1) % shape[longest]
    return result.at[tuple(place)].set(top_value)


def level_of(own_key, dims, cuts, least, largest):
    def one(dim, blocks):
        draws = jax.random.uniform(jax.random.fold_in(jax.random.fold_in(own_key, 6), dim), (blocks,), jnp.float32, least / len(cuts), largest / len(cuts))
        return jnp.repeat(jnp.exp(draws), dims[dim] // blocks).reshape((-1,) + (1,) * (len(dims) - dim - 1))

    loudness = one(*cuts[0])
    for cut in cuts[1:]:
        loudness = loudness * one(*cut)
    return loudness


def deal_out(key, own, number, rows, amount, top, limit, skew):
    sequence = jax.random.permutation(key, amount)
    heavy_load, usual = load_shares(amount, rows * top, limit, skew, True), load_shares(amount, rows * top, limit, skew, False)
    places = jnp.arange(amount)

    def named(lengths, offset_by):
        used = int((lengths > 0).sum())
        fixed = max(1, used // 4)
        moved = fixed + (places - fixed + offset_by * (used - fixed)) % max(1, amount - fixed)
        return jnp.zeros((amount,), jnp.int32).at[sequence[jnp.where(places < fixed, places, moved)]].set(jnp.asarray(lengths, jnp.int32))

    lengths = jnp.where(number % 4 == 0, named(heavy_load, number // 4), named(usual, number - number // 4 - 1))
    mixed = jax.random.permutation(jax.random.fold_in(own, 3), amount)
    donor, receiver = mixed[0:amount // 2 * 2:2], mixed[1:amount // 2 * 2:2]
    margin = jnp.minimum(lengths[donor] - 1, limit - lengths[receiver]) // 2
    margin = jnp.where((donor == sequence[0]) | (receiver == sequence[0]) | (lengths[receiver] == 0), 0, jnp.maximum(margin, 0))
    moved = jax.random.randint(jax.random.fold_in(own, 4), (amount // 2,), 0, 1 << 20) % (margin + 1)
    lengths = lengths.at[donor].add(-moved).at[receiver].add(moved)
    members = jnp.searchsorted(jnp.cumsum(lengths), jnp.arange(rows * top), side="right").astype(jnp.int32)
    table = members.reshape(top, rows).T
    table = table[jax.random.permutation(jax.random.fold_in(own, 1), rows)]
    offset_by = jax.random.randint(jax.random.fold_in(own, 2), (rows, 1), 0, top)
    return jnp.take_along_axis(table, (jnp.arange(top)[None, :] + offset_by) % top, axis=1)


def load_shares(amount, total, bound, lean, full):
    loads = [(1 << 20) // math.isqrt(standing ** lean) + 1 for standing in range(1, amount + 1)]
    largest = bound if full else min(bound, max(-(-total // amount), total * loads[0] // sum(loads)))
    least = 1 if total - largest >= amount - 1 else 0
    counts, spare = [largest] + [least] * (amount - 1), total - largest - least * (amount - 1)
    while spare > 0:
        candidates = [i for i in range(1, amount) if counts[i] < largest] or [i for i in range(1, amount) if counts[i] < bound]
        whole, remaining = sum([loads[i] for i in candidates]), spare
        for i in candidates:
            addition = min(bound - counts[i], max(1, remaining * loads[i] // whole), spare)
            counts[i] = counts[i] + addition
            spare = spare - addition
    return np.array(counts)


def noise(stream_key, shape, width, bound, cuts=(), kind=jnp.bfloat16):
    level = level_of(stream_key, shape, cuts, -0.22, 0.18) if cuts else 1.0
    drawn = jax.random.normal(stream_key, shape, jnp.float32) * width * level
    return jnp.minimum(jnp.maximum(drawn, -bound), bound).astype(kind)


def setup_inputs(seed: int = 0) -> dict:
    splits = jax.random.split(jax.random.key(seed), 7)
    tokens = noise(splits[0], (TOKENS, D), 1.0, 6.0, ((0, 8),))
    expert_ids_keys = jax.random.split(jax.random.fold_in(splits[1], 1), TOKENS // TOK_T)
    expert_ids_turns = jax.random.permutation(jax.random.fold_in(splits[1], 3), TOKENS // TOK_T)
    expert_ids = jax.vmap(lambda own, number: deal_out(jax.random.fold_in(splits[1], 2), own, number, TOK_T, EXPERTS, TOPK, CAPT, 2))(expert_ids_keys, expert_ids_turns).reshape((TOKENS, TOPK))
    gate_units = set_ends(jax.random.randint(splits[2], (TOKENS, TOPK), 1, 65536), jax.random.fold_in(splits[2], 1), 1, 65535).astype(jnp.int32)
    gate_weight = noise(splits[3], (EXPERTS, D, FF), D ** -0.5, 0.078125, ((0, 4), (2, 8)))
    up_weight = noise(splits[4], (EXPERTS, D, FF), D ** -0.5, 0.078125, ((0, 4), (2, 8)))
    down_weight = noise(splits[5], (EXPERTS, D, FF), FF ** -0.5, 0.0625, ((0, 4), (1, 8)))
    return {"tokens": tokens, "expert_ids": expert_ids, "gate_units": gate_units, "gate_weight": gate_weight, "up_weight": up_weight, "down_weight": down_weight}


def slot_tables(expert_ids, gate_units, expert_id, capacity):
    tok_rows = expert_ids.shape[0]
    top_count = expert_ids.shape[1]
    flat_route = expert_ids.reshape(-1)
    matches = (flat_route == expert_id).astype(jnp.int32)
    slot_rank = jnp.cumsum(matches) - matches
    slot_ids = jnp.arange(capacity, dtype=jnp.int32)
    assignment = jnp.where((slot_rank[None, :] == slot_ids[:, None]) & (matches[None, :] == 1), 1.0, 0.0).astype(jnp.float32)
    positions = jnp.arange(tok_rows * top_count, dtype=jnp.int32) // top_count
    owners = (positions[:, None] == jnp.arange(tok_rows, dtype=jnp.int32)[None, :]).astype(jnp.float32)
    unit_vals = gate_units.astype(jnp.float32)
    shares = unit_vals / jnp.sum(unit_vals, axis=1, keepdims=True)
    picker = jnp.dot(assignment, owners, precision=lax.Precision.HIGHEST, preferred_element_type=jnp.float32)
    weighted = jnp.dot(assignment, owners * shares.reshape(-1)[:, None], precision=lax.Precision.HIGHEST, preferred_element_type=jnp.float32)
    return picker, weighted


def reference(tokens, expert_ids, gate_units, gate_weight, up_weight, down_weight):
    block_ids = expert_ids.reshape(N_TENSOR, TOK_T, TOPK)
    block_units = gate_units.reshape(N_TENSOR, TOK_T, TOPK)
    block_tokens = tokens.reshape(N_TENSOR, TOK_T, D).astype(jnp.float32)

    def one_expert(summed, expert_id):
        picker, weighted = jax.vmap(lambda ids, units: slot_tables(ids, units, expert_id, CAPT))(block_ids, block_units)
        picked = jnp.einsum("bct,btd->bcd", picker, block_tokens, precision=lax.Precision.HIGHEST).astype(jnp.bfloat16)
        picked = picked.reshape(N_TENSOR * CAPT, D)
        gate_vals = jnp.dot(picked, gate_weight[expert_id], preferred_element_type=jnp.float32)
        up_vals = jnp.dot(picked, up_weight[expert_id], preferred_element_type=jnp.float32)
        hidden = (jax.nn.silu(gate_vals) * up_vals).astype(jnp.bfloat16)
        projected = jnp.dot(hidden, down_weight[expert_id].T, preferred_element_type=jnp.float32).astype(jnp.bfloat16)
        returned = projected.reshape(N_TENSOR, CAPT, D).astype(jnp.float32)
        contribution = jnp.einsum("bct,bcd->btd", weighted, returned, precision=lax.Precision.HIGHEST)
        return summed + contribution.reshape(TOKENS, D), None

    start_sum = jnp.zeros((TOKENS, D), jnp.float32)
    summed, unused = lax.scan(one_expert, start_sum, jnp.arange(EXPERTS, dtype=jnp.int32))
    return summed.astype(jnp.bfloat16)
```

```python
import jax
import jax.numpy as jnp
from jax import lax
from jax.sharding import PartitionSpec as P


def ring_of(count):
    if count % 2:
        return list(range(count))
    return list(range(0, count, 2)) + list(range(count - 1, 0, -2))


def ring_blocks(block, axis):
    count = lax.axis_size(axis)
    ring = ring_of(count)
    ahead = [(ring[p], ring[(p + 1) % count]) for p in range(count)]
    behind = [(b, a) for a, b in ahead]
    yield 0, block
    forward = backward = block
    for hop in range(1, (count - 1) // 2 + 1):
        forward = lax.ppermute(forward, axis, ahead)
        backward = lax.ppermute(backward, axis, behind)
        yield hop, forward
        yield -hop, backward
    if count % 2 == 0 and count > 1:
        half = block.shape[1] // 2
        first = lax.ppermute(forward[:, :half], axis, ahead)
        second = lax.ppermute(backward[:, half:], axis, behind)
        yield count // 2, (first, second)


def local(tokens, expert_ids, gate_units, gate_weight, up_weight, down_weight):
    experts = lax.axis_size("expert")
    n = lax.axis_size("tensor")
    e = lax.axis_index("expert")
    t = lax.axis_index("tensor")
    rows, width = tokens.shape
    w_gate, w_up, w_down = gate_weight[0], up_weight[0], down_weight[0]
    units = w_gate.shape[1]
    feats = w_down.shape[0]
    ring = jnp.array(ring_of(n), jnp.int32)
    place = jnp.argmax(ring == t).astype(jnp.int32)

    def source(hops):
        return ring[(place - hops) % n]

    part = width // 2
    core = e % 2
    own = lax.dynamic_slice_in_dim(tokens, core * part, part, 1)
    half = jnp.zeros((n, rows, part), tokens.dtype)
    for hops, block in ring_blocks(own, "tensor"):
        if isinstance(block, tuple):
            block = jnp.concatenate(block, 1)
        half = lax.dynamic_update_slice(half, block[None], (source(hops), 0, 0))
    half = half.reshape(n * rows, part)
    other = lax.ppermute(half, "expert", [(i, i ^ 1) for i in range(experts)])

    def dot(a, b):
        return jnp.dot(a, b, preferred_element_type=jnp.float32)

    def project(w):
        mine = lax.dynamic_slice_in_dim(w, core * part, part, 0)
        rest = lax.dynamic_slice_in_dim(w, (1 - core) * part, part, 0)
        return dot(half, mine) + dot(other, rest)

    gate_vals = project(w_gate)
    up_vals = project(w_up)
    hidden = (jax.nn.silu(gate_vals) * up_vals).astype(jnp.bfloat16)

    def down(block, start):
        piece = lax.dynamic_slice_in_dim(w_down, start, block.shape[1], 1)
        return lax.dot_general(
            block, piece, (((1,), (1,)), ((), ())), preferred_element_type=jnp.float32
        )

    projected = jnp.zeros((n * rows, feats), jnp.float32)
    for hops, block in ring_blocks(hidden, "tensor"):
        start = source(hops) * units
        for piece in block if isinstance(block, tuple) else (block,):
            projected = projected + down(piece, start)
            start = start + piece.shape[1]
    outputs = projected.astype(jnp.bfloat16).reshape(n, rows, feats)

    group = n // experts
    units_f = gate_units.astype(jnp.float32)
    shares = units_f / jnp.sum(units_f, axis=1, keepdims=True)
    sums = [jnp.zeros((rows, feats), jnp.float32) for _ in range(group)]
    for k in range(n):
        pairs = []
        for se in range(experts):
            for st in range(n):
                dest = (st // group) * n + (group * se + st % group + k) % n
                pairs.append((se * n + st, dest))
        block = lax.dynamic_index_in_dim(
            outputs, (group * e + t % group + k) % n, 0, keepdims=False
        )
        got = lax.ppermute(block, ("expert", "tensor"), pairs).astype(jnp.float32)
        q = (t - k) % n
        weight = jnp.sum(jnp.where(expert_ids == q // group, shares, 0.0), axis=1)
        for j in range(group):
            sums[j] = sums[j] + jnp.where(q % group == j, weight, 0.0)[:, None] * got
    return jnp.concatenate(sums, axis=1).astype(jnp.bfloat16)


def solution(mesh):
    return jax.shard_map(
        local,
        mesh=mesh,
        in_specs=(
            P("tensor", None),
            P("tensor", None),
            P("tensor", None),
            P("expert", None, "tensor"),
            P("expert", None, "tensor"),
            P("expert", "tensor", None),
        ),
        out_specs=P("tensor", "expert"),
        check_vma=False,
    )
```

```python
import jax
import jax.numpy as jnp
import numpy as np
from jax import lax
from jax.experimental import pallas as pl
from jax.experimental.pallas import tpu as pltpu
from jax.sharding import PartitionSpec as P

LANES = 128
WHOLE = pl.BlockSpec(memory_space=pltpu.VMEM)


def ring_of(count):
    return list(range(0, count, 2)) + list(range(count - 1, 0, -2))


def hop_list(count):
    hops = [0]
    for hop in range(1, count // 2):
        hops += [hop, -hop]
    return hops + [count // 2]


def tables(experts, n):
    ring = ring_of(n)
    hops = hop_list(n)
    group = n // experts
    rows = []
    for e in range(experts):
        for t in range(n):
            place = ring.index(t)
            sources = [ring[(place - hop) % n] for hop in hops]
            mine = [sources.index(group * e + (i + t) % group) for i in range(group)]
            rows.append([e % 2, e, t % group] + sources + mine)
    return np.array(rows, np.int32)


def params(megabytes):
    return pltpu.CompilerParams(vmem_limit_bytes=megabytes << 20)


def dot(a, b):
    return jnp.dot(a, b, preferred_element_type=jnp.float32)


def dot_nt(a, b):
    return lax.dot_general(a, b, (((1,), (1,)), ((), ())), preferred_element_type=jnp.float32)


def first_half(table, x, w_gate, w_up, tile):
    m, part = x.shape[0], w_gate.shape[0] // 2
    units = w_gate.shape[1]
    steps = part // tile

    def kernel(tab, x_ref, g_ref, u_ref, gate, up):
        @pl.when(pl.program_id(0) == 0)
        def _():
            gate[...] = jnp.zeros_like(gate)
            up[...] = jnp.zeros_like(up)

        gate[...] += dot(x_ref[...], g_ref[...])
        up[...] += dot(x_ref[...], u_ref[...])

    weight = pl.BlockSpec((tile, units), lambda k, tab: (tab[0] * steps + k, 0))
    out = jax.ShapeDtypeStruct((m, units), jnp.float32)
    return pl.pallas_call(
        kernel,
        grid_spec=pltpu.PrefetchScalarGridSpec(
            num_scalar_prefetch=1,
            grid=(steps,),
            in_specs=[pl.BlockSpec((m, tile), lambda k, tab: (0, k)), weight, weight],
            out_specs=[WHOLE, WHOLE],
        ),
        out_shape=[out, out],
        compiler_params=params(24),
        cost_estimate=pl.CostEstimate(
            flops=4 * m * part * units, bytes_accessed=4 * part * units, transcendentals=0
        ),
        name="gate_up_own",
    )(table, x, w_gate, w_up)


def second_half(table, x, w_gate, w_up, gate, up, n, tile, j, parts):
    m, part = x.shape[0], w_gate.shape[0] // 2
    units = w_gate.shape[1] // parts
    steps = part // tile
    rows = m // n

    def kernel(tab, x_ref, g_ref, u_ref, gate_in, up_in, out, gate_sum, up_sum):
        k = pl.program_id(0)

        @pl.when(k == 0)
        def _():
            gate_sum[...] = gate_in[...]
            up_sum[...] = up_in[...]

        gate_sum[...] += dot(x_ref[...], g_ref[...])
        up_sum[...] += dot(x_ref[...], u_ref[...])

        @pl.when(k == steps - 1)
        def _():
            for r in range(n):
                piece = pl.ds(r * rows, rows)
                value = gate_sum[piece, :]
                hidden = value * jax.nn.sigmoid(value) * up_sum[piece, :]
                out[tab[3 + r]] = hidden.astype(out.dtype)

    weight = pl.BlockSpec((tile, units), lambda k, tab: ((1 - tab[0]) * steps + k, j))
    sums = pl.BlockSpec((m, units), lambda k, tab: (0, j))
    return pl.pallas_call(
        kernel,
        grid_spec=pltpu.PrefetchScalarGridSpec(
            num_scalar_prefetch=1,
            grid=(steps,),
            in_specs=[pl.BlockSpec((m, tile), lambda k, tab: (0, k)), weight, weight, sums, sums],
            out_specs=WHOLE,
            scratch_shapes=[pltpu.VMEM((m, units), jnp.float32)] * 2,
        ),
        out_shape=jax.ShapeDtypeStruct((n, rows, units), jnp.bfloat16),
        compiler_params=params(24),
        cost_estimate=pl.CostEstimate(
            flops=4 * m * part * units, bytes_accessed=4 * part * units, transcendentals=m * units
        ),
        name="gate_up_other",
    )(table, x, w_gate, w_up, gate, up).reshape(m, units)


def down_step(table, total, blocks, slots, w_down, j, parts):
    m, depth = blocks[0].shape
    feats = w_down.shape[0]
    count = len(blocks)

    def kernel(tab, *refs):
        lhs, w_ref, out = refs[:count], refs[count], refs[-1]
        step = pl.program_id(0)
        for i in range(count):

            @pl.when(step == i)
            def _():
                product = dot_nt(lhs[i][...], w_ref[...])
                if i:
                    out[...] += product
                elif total is None:
                    out[...] = product
                else:
                    out[...] = refs[count + 1][...] + product

    def place(i, tab):
        slot = tab[slots[0]]
        for k in range(1, count):
            slot = jnp.where(i == k, tab[slots[k]], slot)
        return (0, slot * parts + j)

    more = [] if total is None else [total]
    return pl.pallas_call(
        kernel,
        grid_spec=pltpu.PrefetchScalarGridSpec(
            num_scalar_prefetch=1,
            grid=(count,),
            in_specs=[WHOLE] * count + [pl.BlockSpec((feats, depth), place)] + [WHOLE] * len(more),
            out_specs=WHOLE,
        ),
        out_shape=jax.ShapeDtypeStruct((m, feats), jnp.float32),
        compiler_params=params(16),
        cost_estimate=pl.CostEstimate(
            flops=2 * count * m * depth * feats,
            bytes_accessed=2 * count * depth * feats,
            transcendentals=0,
        ),
        name="down",
    )(table, *blocks, w_down, *more)


def down_last(table, total, first, second, slot, w_down, j, parts, experts, final):
    half, depth = first.shape
    m = 2 * half
    feats = w_down.shape[0]
    share = m // experts

    def kernel(tab, a_ref, b_ref, w_ref, total_ref, *outs):
        upper = total_ref[:half, :] + dot_nt(a_ref[...], w_ref[...])
        lower = total_ref[half:, :] + dot_nt(b_ref[...], w_ref[...])
        target = outs[-1]
        target[:half, :] = upper
        target[half:, :] = lower
        if final:
            for i in range(experts):
                start = pl.multiple_of((tab[1] ^ i) * share, share)
                outs[i][...] = target[pl.ds(start, share), :].astype(jnp.bfloat16)

    if final:
        out_shape = [jax.ShapeDtypeStruct((share, feats), jnp.bfloat16)] * experts
        out_specs = [WHOLE] * experts
        scratch = [pltpu.VMEM((m, feats), jnp.float32)]
    else:
        out_shape = jax.ShapeDtypeStruct((m, feats), jnp.float32)
        out_specs = WHOLE
        scratch = []
    return pl.pallas_call(
        kernel,
        grid_spec=pltpu.PrefetchScalarGridSpec(
            num_scalar_prefetch=1,
            grid=(1,),
            in_specs=[
                WHOLE,
                WHOLE,
                pl.BlockSpec((feats, depth), lambda i, tab: (0, tab[slot] * parts + j)),
                WHOLE,
            ],
            out_specs=out_specs,
            scratch_shapes=scratch,
        ),
        out_shape=out_shape,
        compiler_params=params(16),
        cost_estimate=pl.CostEstimate(
            flops=2 * m * depth * feats, bytes_accessed=2 * depth * feats, transcendentals=0
        ),
        name="down_last",
    )(table, first, second, w_down, total)


def combine(table, pieces, routing, n, rows, base):
    experts = len(pieces)
    share, feats = pieces[0].shape
    group = share // rows

    def kernel(tab, *refs):
        ins, route_ref, outs, route = refs[:experts], refs[experts], refs[experts + 1 : -1], refs[-1]
        route[...] = route_ref[...].astype(jnp.float32)
        for k in range(group):
            block = lax.rem(k + tab[2], group)
            info = route[pl.ds(pl.multiple_of(tab[base + k] * rows, rows), rows), :]
            unit0 = info[:, 2:3] * 256.0 + info[:, 3:4]
            unit1 = info[:, 4:5] * 256.0 + info[:, 5:6]
            whole = unit0 + unit1
            share0, share1 = unit0 / whole, unit1 / whole
            mixed = jnp.zeros((rows, feats), jnp.float32)
            for i in range(experts):
                name = (tab[1] ^ i).astype(jnp.float32)
                weight = jnp.where(info[:, 0:1] == name, share0, 0.0)
                weight += jnp.where(info[:, 1:2] == name, share1, 0.0)
                mixed += weight * ins[i][block].astype(jnp.float32)
            outs[k][...] = mixed.astype(jnp.bfloat16)

    last = routing.shape[1] // LANES - 1
    return pl.pallas_call(
        kernel,
        grid_spec=pltpu.PrefetchScalarGridSpec(
            num_scalar_prefetch=1,
            grid=(1,),
            in_specs=[WHOLE] * experts
            + [pl.BlockSpec((n * rows, LANES), lambda i, tab: (0, last))],
            out_specs=[WHOLE] * group,
            scratch_shapes=[pltpu.VMEM((n * rows, LANES), jnp.float32)],
        ),
        out_shape=[jax.ShapeDtypeStruct((rows, feats), jnp.bfloat16)] * group,
        compiler_params=params(16),
        name="combine",
    )(table, *[piece.reshape(group, rows, feats) for piece in pieces], routing)


def assemble(table, pieces):
    group = len(pieces)
    rows, feats = pieces[0].shape

    def kernel(tab, *refs):
        out = refs[-1]
        for k in range(group):
            spot = lax.rem(tab[2] - k + group, group)
            for s in range(group):

                @pl.when(spot == s)
                def _():
                    out[:, s * feats : (s + 1) * feats] = refs[k][...]

    return pl.pallas_call(
        kernel,
        grid_spec=pltpu.PrefetchScalarGridSpec(
            num_scalar_prefetch=1, grid=(1,), in_specs=[WHOLE] * group, out_specs=WHOLE
        ),
        out_shape=jax.ShapeDtypeStruct((rows, group * feats), jnp.bfloat16),
        compiler_params=params(16),
        name="assemble",
    )(table, *pieces)


def local(tokens, expert_ids, gate_units, gate_weight, up_weight, down_weight):
    experts = lax.axis_size("expert")
    n = lax.axis_size("tensor")
    group = n // experts
    rows, width = tokens.shape
    w_gate, w_up, w_down = gate_weight[0], up_weight[0], down_weight[0]
    part = width // 2
    parts = 2 if w_gate.shape[1] % (2 * LANES) == 0 else 1
    tile = next(k for k in (512, 384, 256, 128) if part % k == 0)
    hops = hop_list(n)

    me = lax.axis_index(("expert", "tensor")).astype(jnp.uint32)
    rows_of = jnp.asarray(tables(experts, n))
    length = rows_of.shape[1]
    table = lax.dynamic_slice(rows_of, (me, jnp.uint32(0)), (1, length)).reshape(length)

    ring = ring_of(n)
    ahead = [(ring[p], ring[(p + 1) % n]) for p in range(n)]
    behind = [(b, a) for a, b in ahead]

    high, low = gate_units >> 8, gate_units & 255
    routing = jnp.concatenate(
        [expert_ids, high[:, :1], low[:, :1], high[:, 1:], low[:, 1:]], axis=1
    ).astype(jnp.bfloat16)
    routing = jnp.pad(routing, ((0, 0), (0, LANES - routing.shape[1])))
    core = (lax.axis_index("expert") & 1).astype(jnp.uint32)
    own = lax.dynamic_slice(tokens, (jnp.uint32(0), core * jnp.uint32(part)), (rows, part))
    own = jnp.concatenate([own, routing], axis=1)
    cut = part // (2 * LANES) * LANES
    brought = [own]
    forward = backward = own
    for hop in range(1, n // 2):
        forward = lax.ppermute(forward, "tensor", ahead)
        backward = lax.ppermute(backward, "tensor", behind)
        brought += [forward, backward]
    first = lax.ppermute(forward[:, :cut], "tensor", ahead)
    second = lax.ppermute(backward[:, cut:], "tensor", behind)
    collected = jnp.zeros((n * rows, part + LANES), tokens.dtype)
    for slot, block in enumerate(brought):
        collected = lax.dynamic_update_slice(collected, block, (slot * rows, 0))
    collected = lax.dynamic_update_slice(collected, first, ((n - 1) * rows, 0))
    collected = lax.dynamic_update_slice(collected, second, ((n - 1) * rows, cut))
    other = lax.ppermute(collected, "expert", [(i, i ^ 1) for i in range(experts)])

    gate, up = first_half(table, collected, w_gate, w_up, tile)

    hidden = [
        second_half(table, other, w_gate, w_up, gate, up, n, tile, j, parts) for j in range(parts)
    ]
    total = None
    for j in range(parts):
        total = down_step(table, total, [hidden[j]], [3], w_down, j, parts)
    forward, backward = list(hidden), list(hidden)
    for hop in range(1, n // 2):
        for j in range(parts):
            forward[j] = lax.ppermute(forward[j], "tensor", ahead)
            backward[j] = lax.ppermute(backward[j], "tensor", behind)
            slots = [2 + 2 * hop, 3 + 2 * hop]
            total = down_step(table, total, [forward[j], backward[j]], slots, w_down, j, parts)
    half = n * rows // 2
    for j in range(parts):
        first = lax.ppermute(forward[j][:half], "tensor", ahead)
        second = lax.ppermute(backward[j][half:], "tensor", behind)
        total = down_last(
            table, total, first, second, 2 + n, w_down, j, parts, experts, j == parts - 1
        )

    pieces = [total[0]] + [
        lax.ppermute(total[i], "expert", [(s, s ^ i) for s in range(experts)])
        for i in range(1, experts)
    ]
    mixed = combine(table, pieces, collected, n, rows, 3 + n)
    arrived = []
    for k in range(group):
        pairs = []
        for e in range(experts):
            for t in range(n):
                pairs.append((e * n + t, (t // group) * n + group * e + (k + t) % group))
        arrived.append(lax.ppermute(mixed[k], ("expert", "tensor"), pairs))
    return assemble(table, arrived)


def solution(mesh):
    return jax.shard_map(
        local,
        mesh=mesh,
        in_specs=(
            P("tensor", None),
            P("tensor", None),
            P("tensor", None),
            P("expert", None, "tensor"),
            P("expert", None, "tensor"),
            P("expert", "tensor", None),
        ),
        out_specs=P("tensor", "expert"),
        check_vma=False,
    )
```

```python
import jax
import jax.numpy as jnp
import numpy as np
from jax import lax
from jax.experimental import pallas as pl
from jax.experimental.pallas import tpu as pltpu
from jax.sharding import PartitionSpec as P

LANES = 128
WHOLE = pl.BlockSpec(memory_space=pltpu.VMEM)


def ring_of(count):
    return list(range(0, count, 2)) + list(range(count - 1, 0, -2))


def hop_list(count):
    hops = [0]
    for hop in range(1, count // 2):
        hops += [hop, -hop]
    return hops + [count // 2]


def tables(experts, n):
    ring = ring_of(n)
    hops = hop_list(n)
    group = n // experts
    rows = []
    for e in range(experts):
        for t in range(n):
            place = ring.index(t)
            sources = [ring[(place - hop) % n] for hop in hops]
            mine = [sources.index(group * e + (i + t) % group) for i in range(group)]
            rows.append([e % 2, e, t % group] + sources + mine)
    return np.array(rows, np.int32)


def params(megabytes):
    return pltpu.CompilerParams(vmem_limit_bytes=megabytes << 20)


def dot(a, b):
    return jnp.dot(a, b, preferred_element_type=jnp.float32)


def dot_nt(a, b):
    return lax.dot_general(a, b, (((1,), (1,)), ((), ())), preferred_element_type=jnp.float32)


def fetch(table, weight, other, quarter, after):
    depth, units = weight.shape
    height = depth // 4
    pieces = next(k for k in (4, 2, 1) if height % (k * 16) == 0)
    step = height // pieces

    def kernel(tab, w_ref, after_ref, out, sems):
        del after_ref
        side = 1 - tab[0] if other else tab[0]
        start = pl.multiple_of((2 * side + quarter) * height, height)
        copies = [
            pltpu.make_async_copy(
                w_ref.at[pl.ds(start + i * step, step), :],
                out.at[pl.ds(i * step, step), :],
                sems.at[i],
            )
            for i in range(pieces)
        ]
        for copy in copies:
            copy.start()
        for copy in copies:
            copy.wait()

    return pl.pallas_call(
        kernel,
        grid_spec=pltpu.PrefetchScalarGridSpec(
            num_scalar_prefetch=1,
            in_specs=[
                pl.BlockSpec(memory_space=pltpu.HBM),
                pl.BlockSpec(memory_space=pl.ANY),
            ],
            out_specs=WHOLE,
            scratch_shapes=[pltpu.SemaphoreType.DMA((pieces,))],
        ),
        out_shape=pltpu.VMEM((height, units), weight.dtype),
        compiler_params=params(4),
        cost_estimate=pl.CostEstimate(
            flops=0, bytes_accessed=4 * height * units, transcendentals=0
        ),
        name="fetch",
    )(table, weight, after)


def column_tiles(units):
    size = 256 if units % 256 == 0 else units
    return [slice(i, i + size) for i in range(0, units, size)]


def own_part(x, w_gate, w_up, sums):
    m, (depth, units) = x.shape[0], w_gate.shape

    def kernel(x_ref, g_ref, u_ref, *refs):
        gate, up = refs[-2:]
        for cols in column_tiles(units):
            for w_ref, out, before in ((g_ref, gate, 0), (u_ref, up, 1)):
                product = dot(x_ref[:, :depth], w_ref[:, cols])
                if sums:
                    product += refs[before][:, cols]
                out[:, cols] = product

    out = jax.ShapeDtypeStruct((m, units), jnp.float32)
    return pl.pallas_call(
        kernel,
        in_specs=[WHOLE] * (3 + len(sums)),
        out_specs=[WHOLE, WHOLE],
        out_shape=[out, out],
        compiler_params=params(8),
        cost_estimate=pl.CostEstimate(
            flops=4 * m * depth * units, bytes_accessed=4 * depth * units, transcendentals=0
        ),
        name="gate_up_own",
    )(x, w_gate, w_up, *sums)


def hidden_part(table, xs, gates, ups, sums, n, j, parts):
    m, depth = xs[0].shape[0], gates[0].shape[0]
    units = gates[0].shape[1] // parts
    rows = m // n

    def kernel(tab, x0, x1, g0, g1, u0, u1, gate_ref, up_ref, out):
        for cols in column_tiles(units):
            there = slice(j * units + cols.start, j * units + cols.stop)
            gate = gate_ref[:, there] + dot(x0[:, :depth], g0[:, there])
            up = up_ref[:, there] + dot(x0[:, :depth], u0[:, there])
            gate += dot(x1[:, :depth], g1[:, there])
            up += dot(x1[:, :depth], u1[:, there])
            hidden = (gate * jax.nn.sigmoid(gate) * up).astype(out.dtype)
            for r in range(n):
                out[tab[3 + r], :, cols] = hidden[r * rows : (r + 1) * rows, :]

    return pl.pallas_call(
        kernel,
        grid_spec=pltpu.PrefetchScalarGridSpec(
            num_scalar_prefetch=1, in_specs=[WHOLE] * 8, out_specs=WHOLE
        ),
        out_shape=jax.ShapeDtypeStruct((n, rows, units), jnp.bfloat16),
        compiler_params=params(12),
        cost_estimate=pl.CostEstimate(
            flops=8 * m * depth * units, bytes_accessed=8 * depth * units, transcendentals=m * units
        ),
        name="gate_up_other",
    )(table, *xs, *gates, *ups, *sums).reshape(m, units)


def columns(w_ref, start, buffer, sem):
    depth = buffer.shape[1]
    return pltpu.make_async_copy(
        w_ref.at[:, pl.ds(pl.multiple_of(start * depth, depth), depth)], buffer, sem
    )


def down_step(table, total, blocks, slots, w_down, j, parts):
    m, depth = blocks[0].shape
    feats = w_down.shape[0]
    count = len(blocks)

    def kernel(tab, *refs):
        lhs, w_ref, (out, buffers, sems) = refs[:count], refs[count], refs[-3:]
        copies = [
            columns(w_ref, tab[slots[i]] * parts + j, buffers.at[i], sems.at[i])
            for i in range(count)
        ]
        for copy in copies:
            copy.start()
        for i in range(count):
            copies[i].wait()
            product = dot_nt(lhs[i][...], buffers[i])
            if i:
                out[...] += product
            elif total is None:
                out[...] = product
            else:
                out[...] = refs[count + 1][...] + product

    more = [] if total is None else [total]
    return pl.pallas_call(
        kernel,
        grid_spec=pltpu.PrefetchScalarGridSpec(
            num_scalar_prefetch=1,
            in_specs=[WHOLE] * count + [pl.BlockSpec(memory_space=pltpu.HBM)] + [WHOLE] * len(more),
            out_specs=WHOLE,
            scratch_shapes=[
                pltpu.VMEM((count, feats, depth), w_down.dtype),
                pltpu.SemaphoreType.DMA((count,)),
            ],
        ),
        out_shape=jax.ShapeDtypeStruct((m, feats), jnp.float32),
        compiler_params=params(12),
        cost_estimate=pl.CostEstimate(
            flops=2 * count * m * depth * feats,
            bytes_accessed=2 * count * depth * feats,
            transcendentals=0,
        ),
        name="down",
    )(table, *blocks, w_down, *more)


def down_last(table, total, first, second, slot, w_down, j, parts, experts, final):
    half, depth = first.shape
    m = 2 * half
    feats = w_down.shape[0]
    share = m // experts

    def kernel(tab, a_ref, b_ref, w_ref, total_ref, *refs):
        outs, (target, buffer, sem) = refs[:-3], refs[-3:]
        if not final:
            target = outs[0]
        copy = columns(w_ref, tab[slot] * parts + j, buffer, sem)
        copy.start()
        copy.wait()
        target[:half, :] = total_ref[:half, :] + dot_nt(a_ref[...], buffer[...])
        target[half:, :] = total_ref[half:, :] + dot_nt(b_ref[...], buffer[...])
        if final:
            for i in range(experts):
                start = pl.multiple_of((tab[1] ^ i) * share, share)
                outs[i][...] = target[pl.ds(start, share), :].astype(jnp.bfloat16)

    if final:
        out_shape = [jax.ShapeDtypeStruct((share, feats), jnp.bfloat16)] * experts
        out_specs = [WHOLE] * experts
    else:
        out_shape = jax.ShapeDtypeStruct((m, feats), jnp.float32)
        out_specs = WHOLE
    return pl.pallas_call(
        kernel,
        grid_spec=pltpu.PrefetchScalarGridSpec(
            num_scalar_prefetch=1,
            in_specs=[WHOLE, WHOLE, pl.BlockSpec(memory_space=pltpu.HBM), WHOLE],
            out_specs=out_specs,
            scratch_shapes=[
                pltpu.VMEM((m, feats) if final else (8, LANES), jnp.float32),
                pltpu.VMEM((feats, depth), w_down.dtype),
                pltpu.SemaphoreType.DMA(()),
            ],
        ),
        out_shape=out_shape,
        compiler_params=params(12),
        cost_estimate=pl.CostEstimate(
            flops=2 * m * depth * feats, bytes_accessed=2 * depth * feats, transcendentals=0
        ),
        name="down_last",
    )(table, first, second, w_down, total)


def combine(table, pieces, routing, n, rows, base):
    experts = len(pieces)
    share, feats = pieces[0].shape
    group = share // rows

    def kernel(tab, *refs):
        ins, route_ref, outs, route = refs[:experts], refs[experts], refs[experts + 1 : -1], refs[-1]
        route[...] = route_ref[...].astype(jnp.float32)
        for k in range(group):
            block = lax.rem(k + tab[2], group)
            info = route[pl.ds(pl.multiple_of(tab[base + k] * rows, rows), rows), :]
            unit0 = info[:, 2:3] * 256.0 + info[:, 3:4]
            unit1 = info[:, 4:5] * 256.0 + info[:, 5:6]
            whole = unit0 + unit1
            share0, share1 = unit0 / whole, unit1 / whole
            mixed = jnp.zeros((rows, feats), jnp.float32)
            for i in range(experts):
                name = (tab[1] ^ i).astype(jnp.float32)
                weight = jnp.where(info[:, 0:1] == name, share0, 0.0)
                weight += jnp.where(info[:, 1:2] == name, share1, 0.0)
                mixed += weight * ins[i][block].astype(jnp.float32)
            outs[k][...] = mixed.astype(jnp.bfloat16)

    last = routing.shape[1] // LANES - 1
    return pl.pallas_call(
        kernel,
        grid_spec=pltpu.PrefetchScalarGridSpec(
            num_scalar_prefetch=1,
            grid=(1,),
            in_specs=[WHOLE] * experts
            + [pl.BlockSpec((n * rows, LANES), lambda i, tab: (0, last))],
            out_specs=[WHOLE] * group,
            scratch_shapes=[pltpu.VMEM((n * rows, LANES), jnp.float32)],
        ),
        out_shape=[jax.ShapeDtypeStruct((rows, feats), jnp.bfloat16)] * group,
        compiler_params=params(16),
        name="combine",
    )(table, *[piece.reshape(group, rows, feats) for piece in pieces], routing)


def assemble(table, pieces):
    group = len(pieces)
    rows, feats = pieces[0].shape

    def kernel(tab, *refs):
        out = refs[-1]
        for k in range(group):
            spot = lax.rem(tab[2] - k + group, group)
            for s in range(group):

                @pl.when(spot == s)
                def _():
                    out[:, s * feats : (s + 1) * feats] = refs[k][...]

    return pl.pallas_call(
        kernel,
        grid_spec=pltpu.PrefetchScalarGridSpec(
            num_scalar_prefetch=1, grid=(1,), in_specs=[WHOLE] * group, out_specs=WHOLE
        ),
        out_shape=jax.ShapeDtypeStruct((rows, group * feats), jnp.bfloat16),
        compiler_params=params(16),
        name="assemble",
    )(table, *pieces)


def local(tokens, expert_ids, gate_units, gate_weight, up_weight, down_weight):
    experts = lax.axis_size("expert")
    n = lax.axis_size("tensor")
    group = n // experts
    rows, width = tokens.shape
    w_gate, w_up, w_down = (
        pltpu.with_memory_space_constraint(w[0], pltpu.HBM)
        for w in (gate_weight, up_weight, down_weight)
    )
    part = width // 2
    parts = 2 if w_gate.shape[1] % (2 * LANES) == 0 else 1

    me = lax.axis_index(("expert", "tensor")).astype(jnp.uint32)
    rows_of = jnp.asarray(tables(experts, n))
    length = rows_of.shape[1]
    table = lax.dynamic_slice(rows_of, (me, jnp.uint32(0)), (1, length)).reshape(length)

    ring = ring_of(n)
    ahead = [(ring[p], ring[(p + 1) % n]) for p in range(n)]
    behind = [(b, a) for a, b in ahead]

    high, low = gate_units >> 8, gate_units & 255
    routing = jnp.concatenate(
        [expert_ids, high[:, :1], low[:, :1], high[:, 1:], low[:, 1:]], axis=1
    ).astype(jnp.bfloat16)
    routing = jnp.pad(routing, ((0, 0), (0, LANES - routing.shape[1])))
    core = (lax.axis_index("expert") & 1).astype(jnp.uint32)
    quarter = part // 2
    starts = []
    for q in range(2):
        where = core * jnp.uint32(part) + jnp.uint32(q * quarter)
        starts.append(lax.dynamic_slice(tokens, (jnp.uint32(0), where), (rows, quarter)))
    starts[1] = jnp.concatenate([starts[1], routing], axis=1)

    wanted = [(o, q, w) for o in (False, True) for q in range(2) for w in (w_gate, w_up)]
    fetched = []

    def fetch_next(count, after):
        for o, q, w in wanted[len(fetched) : len(fetched) + count]:
            fetched.append(fetch(table, w, o, q, after))

    brought = [[block] for block in starts]
    forward, backward = list(starts), list(starts)
    cut = quarter // (2 * LANES) * LANES
    for hop in range(1, n // 2 + 1):
        for q in range(2):
            if hop > 1:
                forward[q], backward[q], fetched[-2:] = lax.optimization_barrier(
                    (forward[q], backward[q], fetched[-2:])
                )
            fetch_next(1, forward[q])
            if hop < n // 2:
                forward[q] = lax.ppermute(forward[q], "tensor", ahead)
                backward[q] = lax.ppermute(backward[q], "tensor", behind)
                brought[q] += [forward[q], backward[q]]
            else:
                first = lax.ppermute(forward[q][:, :cut], "tensor", ahead)
                second = lax.ppermute(backward[q][:, cut:], "tensor", behind)
                brought[q].append(jnp.concatenate([first, second], axis=1))
    fetch_next(len(wanted), forward[1])
    gates, ups = fetched[0::2], fetched[1::2]

    sums = []
    collected, other = [], []
    for q in range(2):
        whole = jnp.zeros((n * rows, starts[q].shape[1]), tokens.dtype)
        for slot, block in enumerate(brought[q]):
            whole = lax.dynamic_update_slice(whole, block, (slot * rows, 0))
        collected.append(whole)
        other.append(lax.ppermute(whole, "expert", [(i, i ^ 1) for i in range(experts)]))
        sums = own_part(whole, gates[q], ups[q], sums)

    hidden = [
        hidden_part(table, other, gates[2:], ups[2:], sums, n, j, parts) for j in range(parts)
    ]
    total = None
    held = [([block], [3]) for block in hidden]
    half = n * rows // 2
    last = []
    for hop in range(1, n // 2 + 1):
        for j in range(parts):
            blocks, slots = held[j]
            if total is not None:
                blocks, total = lax.optimization_barrier((blocks, total))
            forward, backward = blocks[0], blocks[-1]
            if hop < n // 2:
                forward = lax.ppermute(forward, "tensor", ahead)
                backward = lax.ppermute(backward, "tensor", behind)
                held[j] = ([forward, backward], [2 + 2 * hop, 3 + 2 * hop])
            else:
                forward = lax.ppermute(forward[:half], "tensor", ahead)
                backward = lax.ppermute(backward[half:], "tensor", behind)
                last.append((forward, backward))
            total = down_step(table, total, blocks, slots, w_down, j, parts)
    for j in range(parts):
        total = down_last(table, total, *last[j], 2 + n, w_down, j, parts, experts, j == parts - 1)

    pieces = [total[0]] + [
        lax.ppermute(total[i], "expert", [(s, s ^ i) for s in range(experts)])
        for i in range(1, experts)
    ]
    mixed = combine(table, pieces, collected[1], n, rows, 3 + n)
    arrived = []
    for k in range(group):
        pairs = []
        for e in range(experts):
            for t in range(n):
                pairs.append((e * n + t, (t // group) * n + group * e + (k + t) % group))
        arrived.append(lax.ppermute(mixed[k], ("expert", "tensor"), pairs))
    return assemble(table, arrived)


def solution(mesh):
    return jax.shard_map(
        local,
        mesh=mesh,
        in_specs=(
            P("tensor", None),
            P("tensor", None),
            P("tensor", None),
            P("expert", None, "tensor"),
            P("expert", None, "tensor"),
            P("expert", "tensor", None),
        ),
        out_specs=P("tensor", "expert"),
        check_vma=False,
    )
```

```python
import jax
import jax.numpy as jnp
import numpy as np
from jax import lax
from jax.experimental import pallas as pl
from jax.experimental.pallas import tpu as pltpu
from jax.sharding import PartitionSpec as P

LANES = 128
WHOLE = pl.BlockSpec(memory_space=pltpu.VMEM)


def ring_of(count):
    return list(range(0, count, 2)) + list(range(count - 1, 0, -2))


def hop_list(count):
    hops = [0]
    for hop in range(1, count // 2):
        hops += [hop, -hop]
    return hops + [count // 2]


def tables(experts, n):
    ring = ring_of(n)
    hops = hop_list(n)
    group = n // experts
    rows = []
    for e in range(experts):
        for t in range(n):
            place = ring.index(t)
            sources = [ring[(place - hop) % n] for hop in hops]
            mine = [sources.index(group * e + (i + t) % group) for i in range(group)]
            rows.append([e % 2, e, t % group] + sources + mine)
    return np.array(rows, np.int32)


def params(megabytes):
    return pltpu.CompilerParams(vmem_limit_bytes=megabytes << 20)


def dot(a, b):
    return jnp.dot(a, b, preferred_element_type=jnp.float32)


def dot_nt(a, b):
    return lax.dot_general(a, b, (((1,), (1,)), ((), ())), preferred_element_type=jnp.float32)


def prepare(core, tokens, expert_ids, gate_units):
    rows, width = tokens.shape
    part = width // 2

    def kernel(core_ref, tokens_ref, ids_ref, units_ref, out, ids, units, sems):
        start = pl.multiple_of(core_ref[0] * part, part)
        copies = [
            pltpu.make_async_copy(source, target, sems.at[i])
            for i, (source, target) in enumerate(
                [
                    (ids_ref, ids),
                    (units_ref, units),
                    (tokens_ref.at[:, pl.ds(start, part)], out.at[:, :part]),
                ]
            )
        ]
        for copy in copies:
            copy.start()
        copies[0].wait()
        copies[1].wait()
        number = units[...]
        lines = [ids[...], number >> 8, number & 255]
        route = jnp.concatenate(
            [line.astype(jnp.float32) for line in lines] + [jnp.zeros((2, rows), jnp.float32)], axis=0
        )
        route = jnp.concatenate([route, jnp.zeros((8, LANES - rows), jnp.float32)], axis=1)
        route = jnp.concatenate([route, jnp.zeros((LANES - 8, LANES), jnp.float32)], axis=0)
        out[:, part:] = route.T[:rows, :].astype(jnp.bfloat16)
        copies[2].wait()

    hbm = pl.BlockSpec(memory_space=pltpu.HBM)
    return pl.pallas_call(
        kernel,
        grid_spec=pltpu.PrefetchScalarGridSpec(
            num_scalar_prefetch=1,
            in_specs=[hbm] * 3,
            out_specs=WHOLE,
            scratch_shapes=[
                pltpu.VMEM((2, rows), jnp.int32),
                pltpu.VMEM((2, rows), jnp.int32),
                pltpu.SemaphoreType.DMA((3,)),
            ],
        ),
        out_shape=pltpu.VMEM((rows, part + LANES), tokens.dtype),
        compiler_params=params(4),
        name="prepare",
    )(core, *[pltpu.with_memory_space_constraint(a, pltpu.HBM) for a in (tokens, expert_ids, gate_units)])


def bring(w_ref, out, sems, rows, columns):
    pieces = sems.shape[0]
    step = out.shape[0] // pieces
    copies = []
    for i in range(pieces):
        start = rows + i * step
        if not isinstance(start, int):
            start = pl.multiple_of(start, step)
        copies.append(
            pltpu.make_async_copy(
                w_ref.at[pl.ds(start, step), columns], out.at[pl.ds(i * step, step), :], sems.at[i]
            )
        )
    for copy in copies:
        copy.start()
    for copy in copies:
        copy.wait()


def fetch(table, weight, shape, place, after):
    pieces = next(k for k in (8, 4, 2, 1) if shape[0] % (k * 16) == 0)

    def kernel(tab, w_ref, after_ref, out, sems):
        del after_ref
        bring(w_ref, out, sems, *place(tab))

    return pl.pallas_call(
        kernel,
        grid_spec=pltpu.PrefetchScalarGridSpec(
            num_scalar_prefetch=1,
            in_specs=[
                pl.BlockSpec(memory_space=pltpu.HBM),
                pl.BlockSpec(memory_space=pl.ANY),
            ],
            out_specs=WHOLE,
            scratch_shapes=[pltpu.SemaphoreType.DMA((pieces,))],
        ),
        out_shape=pltpu.VMEM(shape, weight.dtype),
        compiler_params=params(4),
        cost_estimate=pl.CostEstimate(
            flops=0, bytes_accessed=4 * shape[0] * shape[1], transcendentals=0
        ),
        name="fetch",
    )(table, weight, after)


def column_tiles(units):
    size = 256 if units % 256 == 0 else units
    return [slice(i, i + size) for i in range(0, units, size)]


def depth_part(x, w_gate, w_up, q, sums):
    m, depth = x.shape
    units = w_gate.shape[1]
    rows = slice(q * depth, (q + 1) * depth)

    def kernel(x_ref, g_ref, u_ref, *refs):
        gate, up = refs[-2:]
        for cols in column_tiles(units):
            for w_ref, out, before in ((g_ref, gate, 0), (u_ref, up, 1)):
                product = dot(x_ref[...], w_ref[rows, cols])
                if sums:
                    product += refs[before][:, cols]
                out[:, cols] = product

    out = jax.ShapeDtypeStruct((m, units), jnp.float32)
    return pl.pallas_call(
        kernel,
        in_specs=[WHOLE] * (3 + len(sums)),
        out_specs=[WHOLE, WHOLE],
        out_shape=[out, out],
        compiler_params=params(8),
        cost_estimate=pl.CostEstimate(
            flops=4 * m * depth * units, bytes_accessed=4 * depth * units, transcendentals=0
        ),
        name="gate_up",
    )(x, w_gate, w_up, *sums)


def hidden_part(table, x, w_gate, w_up, q, sums, n, j, parts):
    m, depth = x.shape
    units = w_gate.shape[1] // parts
    rows = m // n
    deep = slice(q * depth, (q + 1) * depth)

    def kernel(tab, x_ref, g_ref, u_ref, gate_ref, up_ref, out):
        for cols in column_tiles(units):
            there = slice(j * units + cols.start, j * units + cols.stop)
            gate = gate_ref[:, there] + dot(x_ref[...], g_ref[deep, there])
            up = up_ref[:, there] + dot(x_ref[...], u_ref[deep, there])
            hidden = (gate * jax.nn.sigmoid(gate) * up).astype(out.dtype)
            for r in range(n):
                out[tab[3 + r], :, cols] = hidden[r * rows : (r + 1) * rows, :]

    return pl.pallas_call(
        kernel,
        grid_spec=pltpu.PrefetchScalarGridSpec(
            num_scalar_prefetch=1, in_specs=[WHOLE] * 5, out_specs=WHOLE
        ),
        out_shape=jax.ShapeDtypeStruct((n, rows, units), jnp.bfloat16),
        compiler_params=params(12),
        cost_estimate=pl.CostEstimate(
            flops=4 * m * depth * units, bytes_accessed=4 * depth * units, transcendentals=m * units
        ),
        name="hidden",
    )(table, x, w_gate, w_up, *sums).reshape(m, units)


def columns(w_ref, start, buffer, sem):
    depth = buffer.shape[1]
    return pltpu.make_async_copy(
        w_ref.at[:, pl.ds(pl.multiple_of(start * depth, depth), depth)], buffer, sem
    )


def down_step(table, total, blocks, places, w_down, parts):
    m, depth = blocks[0].shape
    feats = w_down.shape[0]
    count = len(blocks)

    def kernel(tab, *refs):
        lhs, w_ref, (out, buffers, sems) = refs[:count], refs[count], refs[-3:]
        copies = [
            columns(w_ref, tab[slot] * parts + j, buffers.at[i], sems.at[i])
            for i, (slot, j) in enumerate(places)
        ]
        for copy in copies:
            copy.start()
        for i in range(count):
            copies[i].wait()
            product = dot_nt(lhs[i][...], buffers[i])
            if i:
                out[...] += product
            elif total is None:
                out[...] = product
            else:
                out[...] = refs[count + 1][...] + product

    more = [] if total is None else [total]
    return pl.pallas_call(
        kernel,
        grid_spec=pltpu.PrefetchScalarGridSpec(
            num_scalar_prefetch=1,
            in_specs=[WHOLE] * count + [pl.BlockSpec(memory_space=pltpu.HBM)] + [WHOLE] * len(more),
            out_specs=WHOLE,
            scratch_shapes=[
                pltpu.VMEM((count, feats, depth), w_down.dtype),
                pltpu.SemaphoreType.DMA((count,)),
            ],
        ),
        out_shape=jax.ShapeDtypeStruct((m, feats), jnp.float32),
        compiler_params=params(12),
        cost_estimate=pl.CostEstimate(
            flops=2 * count * m * depth * feats,
            bytes_accessed=2 * count * depth * feats,
            transcendentals=0,
        ),
        name="down",
    )(table, *blocks, w_down, *more)


def down_last(table, total, first, second, w_last, j, experts, final):
    half, depth = first.shape
    m = 2 * half
    feats = w_last.shape[0]
    share = m // experts
    there = slice(j * depth, (j + 1) * depth)

    def kernel(tab, a_ref, b_ref, w_ref, total_ref, *refs):
        target = refs[-1] if final else refs[0]
        target[:half, :] = total_ref[:half, :] + dot_nt(a_ref[...], w_ref[:, there])
        target[half:, :] = total_ref[half:, :] + dot_nt(b_ref[...], w_ref[:, there])
        if final:
            for i in range(experts):
                start = pl.multiple_of((tab[1] ^ i) * share, share)
                refs[i][...] = target[pl.ds(start, share), :].astype(jnp.bfloat16)

    if final:
        out_shape = [jax.ShapeDtypeStruct((share, feats), jnp.bfloat16)] * experts
        out_specs = [WHOLE] * experts
    else:
        out_shape = jax.ShapeDtypeStruct((m, feats), jnp.float32)
        out_specs = WHOLE
    return pl.pallas_call(
        kernel,
        grid_spec=pltpu.PrefetchScalarGridSpec(
            num_scalar_prefetch=1,
            in_specs=[WHOLE] * 4,
            out_specs=out_specs,
            scratch_shapes=[pltpu.VMEM((m, feats), jnp.float32)] if final else [],
        ),
        out_shape=out_shape,
        compiler_params=params(12),
        cost_estimate=pl.CostEstimate(
            flops=2 * m * depth * feats, bytes_accessed=2 * depth * feats, transcendentals=0
        ),
        name="down_last",
    )(table, first, second, w_last, total)


def combine(table, pieces, routing, n, base):
    experts = len(pieces)
    share, feats = pieces[0].shape
    rows = routing.shape[0] // n
    group = share // rows

    def kernel(tab, *refs):
        ins, route_ref, outs, route = refs[:experts], refs[experts], refs[experts + 1 : -1], refs[-1]
        route[...] = route_ref[...].astype(jnp.float32)
        for k in range(group):
            block = lax.rem(k + tab[2], group)
            info = route[pl.ds(pl.multiple_of(tab[base + k] * rows, rows), rows), :]
            unit0 = info[:, 2:3] * 256.0 + info[:, 4:5]
            unit1 = info[:, 3:4] * 256.0 + info[:, 5:6]
            whole = unit0 + unit1
            share0, share1 = unit0 / whole, unit1 / whole
            mixed = jnp.zeros((rows, feats), jnp.float32)
            for i in range(experts):
                name = (tab[1] ^ i).astype(jnp.float32)
                weight = jnp.where(info[:, 0:1] == name, share0, 0.0)
                weight += jnp.where(info[:, 1:2] == name, share1, 0.0)
                mixed += weight * ins[i][block].astype(jnp.float32)
            outs[k][...] = mixed.astype(jnp.bfloat16)

    return pl.pallas_call(
        kernel,
        grid_spec=pltpu.PrefetchScalarGridSpec(
            num_scalar_prefetch=1,
            in_specs=[WHOLE] * (experts + 1),
            out_specs=[WHOLE] * group,
            scratch_shapes=[pltpu.VMEM(routing.shape, jnp.float32)],
        ),
        out_shape=[jax.ShapeDtypeStruct((rows, feats), jnp.bfloat16)] * group,
        compiler_params=params(16),
        name="combine",
    )(table, *[piece.reshape(group, rows, feats) for piece in pieces], routing)


def assemble(table, pieces):
    group = len(pieces)
    rows, feats = pieces[0].shape

    def kernel(tab, *refs):
        out = refs[-1]
        for k in range(group):
            spot = lax.rem(tab[2] - k + group, group)
            for s in range(group):

                @pl.when(spot == s)
                def _():
                    out[:, s * feats : (s + 1) * feats] = refs[k][...]

    return pl.pallas_call(
        kernel,
        grid_spec=pltpu.PrefetchScalarGridSpec(
            num_scalar_prefetch=1, grid=(1,), in_specs=[WHOLE] * group, out_specs=WHOLE
        ),
        out_shape=jax.ShapeDtypeStruct((rows, group * feats), jnp.bfloat16),
        compiler_params=params(16),
        name="assemble",
    )(table, *pieces)


def local(tokens, expert_ids, gate_units, gate_weight, up_weight, down_weight):
    experts = lax.axis_size("expert")
    n = lax.axis_size("tensor")
    group = n // experts
    rows, width = tokens.shape
    w_gate, w_up, w_down = (
        pltpu.with_memory_space_constraint(w[0], pltpu.HBM)
        for w in (gate_weight, up_weight, down_weight)
    )
    part = width // 2
    parts = 2 if w_gate.shape[1] % (2 * LANES) == 0 else 1

    me = lax.axis_index(("expert", "tensor")).astype(jnp.uint32)
    rows_of = jnp.asarray(tables(experts, n))
    length = rows_of.shape[1]
    table = lax.dynamic_slice(rows_of, (me, jnp.uint32(0)), (1, length)).reshape(length)

    ring = ring_of(n)
    ahead = [(ring[p], ring[(p + 1) % n]) for p in range(n)]
    behind = [(b, a) for a, b in ahead]

    core = (lax.axis_index("expert") & 1).reshape(1)
    own = prepare(core, tokens, expert_ids.T, gate_units.T)
    wanted = [(other, w) for other in (False, True) for w in (w_gate, w_up)]
    fetched = []

    def fetch_next(after):
        other, w = wanted[len(fetched)]

        def place(tab):
            return (1 - tab[0] if other else tab[0]) * part, slice(None)

        fetched.append(fetch(table, w, (part, w.shape[1]), place, after))

    brought = [own]
    forward = backward = own
    cut = part // 2
    for hop in range(1, n // 2 + 1):
        if hop > 1 and len(fetched) < len(wanted) + 1:
            forward, backward, fetched[-1] = lax.optimization_barrier(
                (forward, backward, fetched[-1])
            )
        if len(fetched) < len(wanted):
            fetch_next(forward)
        if hop < n // 2:
            forward = lax.ppermute(forward, "tensor", ahead)
            backward = lax.ppermute(backward, "tensor", behind)
            brought += [forward, backward]
        else:
            first = lax.ppermute(forward[:, :cut], "tensor", ahead)
            second = lax.ppermute(backward[:, cut:], "tensor", behind)
    while len(fetched) < len(wanted):
        fetch_next(forward)

    first, second, fetched[-1] = lax.optimization_barrier((first, second, fetched[-1]))
    far = jnp.concatenate([first, second], axis=1)
    collected, other = [], []
    for cols in (slice(0, cut), slice(cut, part), slice(part, part + LANES)):
        whole = jnp.zeros((n * rows, cols.stop - cols.start), tokens.dtype)
        for slot, block in enumerate(brought + [far]):
            whole = lax.dynamic_update_slice(whole, block[:, cols], (slot * rows, 0))
        collected.append(whole)
    gate_own, up_own, gate_other, up_other = fetched
    routing = collected[2]
    for q in range(2):
        other.append(lax.ppermute(collected[q], "expert", [(i, i ^ 1) for i in range(experts)]))
    sums = []
    for q in range(2):
        sums = depth_part(collected[q], gate_own, up_own, q, sums)
    sums = depth_part(other[0], gate_other, up_other, 0, sums)

    hidden = [
        hidden_part(table, other[1], gate_other, up_other, 1, sums, n, j, parts)
        for j in range(parts)
    ]
    total = None
    held = [([block], [3]) for block in hidden]
    half = n * rows // 2
    units = w_down.shape[1] // n
    w_last = None
    for hop in range(1, n // 2 + 1):
        came = []
        for j in range(parts):
            blocks, slots = held[j]
            if j == 0 and total is not None:
                blocks, total = lax.optimization_barrier((blocks, total))
            forward, backward = blocks[0], blocks[-1]
            if hop < n // 2:
                forward = lax.ppermute(forward, "tensor", ahead)
                backward = lax.ppermute(backward, "tensor", behind)
                held[j] = ([forward, backward], [2 + 2 * hop, 3 + 2 * hop])
            else:
                forward = lax.ppermute(forward[:half], "tensor", ahead)
                backward = lax.ppermute(backward[half:], "tensor", behind)
                held[j] = (forward, backward)
            came += [(block, (slot, j)) for block, slot in zip(blocks, slots)]
        total = down_step(table, total, [c[0] for c in came], [c[1] for c in came], w_down, parts)
        if w_last is None:
            w_last = fetch(
                table,
                w_down,
                (w_down.shape[0], units),
                lambda tab: (0, pl.ds(pl.multiple_of(tab[2 + n] * units, units), units)),
                hidden[-1],
            )
            total, w_last = lax.optimization_barrier((total, w_last))
    for j in range(parts):
        total = down_last(table, total, *held[j], w_last, j, experts, j == parts - 1)

    pieces = [total[0]] + [
        lax.ppermute(total[i], "expert", [(s, s ^ i) for s in range(experts)])
        for i in range(1, experts)
    ]
    mixed = combine(table, pieces, routing, n, 3 + n)
    arrived = []
    for k in range(group):
        pairs = []
        for e in range(experts):
            for t in range(n):
                pairs.append((e * n + t, (t // group) * n + group * e + (k + t) % group))
        arrived.append(lax.ppermute(mixed[k], ("expert", "tensor"), pairs))
    return assemble(table, arrived)


def solution(mesh):
    return jax.shard_map(
        local,
        mesh=mesh,
        in_specs=(
            P("tensor", None),
            P("tensor", None),
            P("tensor", None),
            P("expert", None, "tensor"),
            P("expert", None, "tensor"),
            P("expert", "tensor", None),
        ),
        out_specs=P("tensor", "expert"),
        check_vma=False,
    )
```

```python
import jax
import jax.numpy as jnp
import numpy as np
from jax import lax
from jax.experimental import pallas as pl
from jax.experimental.pallas import tpu as pltpu
from jax.sharding import PartitionSpec as P

LANES = 128
WHOLE = pl.BlockSpec(memory_space=pltpu.VMEM)


def ring_of(count):
    return list(range(0, count, 2)) + list(range(count - 1, 0, -2))


def hop_list(count):
    hops = [0]
    for hop in range(1, count // 2):
        hops += [hop, -hop]
    return hops + [count // 2]


def tables(experts, n):
    ring = ring_of(n)
    hops = hop_list(n)
    group = n // experts
    rows = []
    for e in range(experts):
        for t in range(n):
            place = ring.index(t)
            sources = [ring[(place - hop) % n] for hop in hops]
            mine = [sources.index(group * e + (i + t) % group) for i in range(group)]
            rows.append([e % 2, e, t % group] + sources + mine)
    return np.array(rows, np.int32)


def params(megabytes):
    return pltpu.CompilerParams(vmem_limit_bytes=megabytes << 20)


def dot(a, b):
    return jnp.dot(a, b, preferred_element_type=jnp.float32)


def dot_nt(a, b):
    return lax.dot_general(a, b, (((1,), (1,)), ((), ())), preferred_element_type=jnp.float32)


def prepare(core, tokens, expert_ids, gate_units):
    rows, width = tokens.shape
    part = width // 2
    cut = part // 2

    def kernel(core_ref, tokens_ref, ids_ref, units_ref, low, high, ids, units, sems):
        start = pl.multiple_of(core_ref[0] * part, part)
        copies = [
            pltpu.make_async_copy(source, target, sems.at[i])
            for i, (source, target) in enumerate(
                [
                    (ids_ref, ids),
                    (units_ref, units),
                    (tokens_ref.at[:, pl.ds(start, cut)], low),
                    (tokens_ref.at[:, pl.ds(start + cut, cut)], high.at[:, :cut]),
                ]
            )
        ]
        for copy in copies:
            copy.start()
        copies[0].wait()
        copies[1].wait()
        number = units[...]
        lines = [ids[...], number >> 8, number & 255]
        route = jnp.concatenate(
            [line.astype(jnp.float32) for line in lines] + [jnp.zeros((2, rows), jnp.float32)], axis=0
        )
        route = jnp.concatenate([route, jnp.zeros((8, LANES - rows), jnp.float32)], axis=1)
        route = jnp.concatenate([route, jnp.zeros((LANES - 8, LANES), jnp.float32)], axis=0)
        high[:, cut:] = route.T[:rows, :].astype(jnp.bfloat16)
        copies[2].wait()
        copies[3].wait()

    hbm = pl.BlockSpec(memory_space=pltpu.HBM)
    return pl.pallas_call(
        kernel,
        grid_spec=pltpu.PrefetchScalarGridSpec(
            num_scalar_prefetch=1,
            in_specs=[hbm] * 3,
            out_specs=[WHOLE, WHOLE],
            scratch_shapes=[
                pltpu.VMEM((2, rows), jnp.int32),
                pltpu.VMEM((2, rows), jnp.int32),
                pltpu.SemaphoreType.DMA((4,)),
            ],
        ),
        out_shape=[
            pltpu.VMEM((rows, cut), tokens.dtype),
            pltpu.VMEM((rows, cut + LANES), tokens.dtype),
        ],
        compiler_params=params(4),
        name="prepare",
    )(core, *[pltpu.with_memory_space_constraint(a, pltpu.HBM) for a in (tokens, expert_ids, gate_units)])


def depth_part(table, x, w_gate, w_up, q, sums, tile):
    m, depth = x.shape
    units = w_gate.shape[1]
    steps = depth // tile

    def kernel(tab, x_ref, g_ref, u_ref, *refs):
        gate, up = refs[-2:]
        for w_ref, out, before in ((g_ref, gate, 0), (u_ref, up, 1)):
            product = dot(x_ref[...], w_ref[...])

            @pl.when(pl.program_id(0) == 0)
            def _():
                out[...] = product + refs[before][...] if sums else product

            @pl.when(pl.program_id(0) > 0)
            def _():
                out[...] += product

    weight = pl.BlockSpec((tile, units), lambda k, tab: ((2 * tab[0] + q) * steps + k, 0))
    out = jax.ShapeDtypeStruct((m, units), jnp.float32)
    return pl.pallas_call(
        kernel,
        grid_spec=pltpu.PrefetchScalarGridSpec(
            num_scalar_prefetch=1,
            grid=(steps,),
            in_specs=[pl.BlockSpec((m, tile), lambda k, tab: (0, k)), weight, weight]
            + [WHOLE] * len(sums),
            out_specs=[WHOLE, WHOLE],
        ),
        out_shape=[out, out],
        compiler_params=params(16),
        cost_estimate=pl.CostEstimate(
            flops=4 * m * depth * units, bytes_accessed=4 * depth * units, transcendentals=0
        ),
        name="gate_up",
    )(table, x, w_gate, w_up, *sums)


def hidden_part(table, xs, w_gate, w_up, sums, n, j, parts, tile):
    m, depth = xs[0].shape
    units = w_gate.shape[1] // parts
    rows = m // n
    steps = depth // tile

    def kernel(tab, x0, x1, g_ref, u_ref, gate_in, up_in, out, gate, up):
        k = pl.program_id(0)

        def add(x_ref, first):
            for w_ref, total, before in ((g_ref, gate, gate_in), (u_ref, up, up_in)):
                total[...] = (before if first else total)[...] + dot(x_ref[...], w_ref[...])

        pl.when(k == 0)(lambda: add(x0, True))
        pl.when((k > 0) & (k < steps))(lambda: add(x0, False))
        pl.when(k >= steps)(lambda: add(x1, False))

        @pl.when(k == 2 * steps - 1)
        def _():
            for r in range(n):
                piece = slice(r * rows, (r + 1) * rows)
                value = gate[piece, :]
                hidden = value * jax.nn.sigmoid(value) * up[piece, :]
                out[tab[3 + r]] = hidden.astype(out.dtype)

    weight = pl.BlockSpec((tile, units), lambda k, tab: (2 * (1 - tab[0]) * steps + k, j))
    part_sum = pl.BlockSpec((m, units), lambda k, tab: (0, j))
    return pl.pallas_call(
        kernel,
        grid_spec=pltpu.PrefetchScalarGridSpec(
            num_scalar_prefetch=1,
            grid=(2 * steps,),
            in_specs=[
                pl.BlockSpec((m, tile), lambda k, tab: (0, jnp.minimum(k, steps - 1))),
                pl.BlockSpec((m, tile), lambda k, tab: (0, jnp.maximum(k - steps, 0))),
                weight,
                weight,
                part_sum,
                part_sum,
            ],
            out_specs=WHOLE,
            scratch_shapes=[pltpu.VMEM((m, units), jnp.float32)] * 2,
        ),
        out_shape=jax.ShapeDtypeStruct((n, rows, units), jnp.bfloat16),
        compiler_params=params(16),
        cost_estimate=pl.CostEstimate(
            flops=8 * m * depth * units, bytes_accessed=8 * depth * units, transcendentals=m * units
        ),
        name="hidden",
    )(table, *xs, w_gate, w_up, *sums).reshape(m, units)


def down_step(table, total, blocks, places, w_down, parts):
    m, depth = blocks[0].shape
    feats = w_down.shape[0]
    count = len(blocks)

    def kernel(tab, *refs):
        lhs, w_ref, out = refs[:count], refs[count], refs[-1]
        for i, (slot, j) in enumerate(places):
            start = pl.multiple_of((tab[slot] * parts + j) * depth, depth)
            product = dot_nt(lhs[i][...], w_ref[:, pl.ds(start, depth)])
            if i:
                out[...] += product
            elif total is None:
                out[...] = product
            else:
                out[...] = refs[count + 1][...] + product

    more = [] if total is None else [total]
    return pl.pallas_call(
        kernel,
        grid_spec=pltpu.PrefetchScalarGridSpec(
            num_scalar_prefetch=1,
            in_specs=[WHOLE] * (count + 1 + len(more)),
            out_specs=WHOLE,
        ),
        out_shape=jax.ShapeDtypeStruct((m, feats), jnp.float32),
        compiler_params=params(8),
        cost_estimate=pl.CostEstimate(
            flops=2 * count * m * depth * feats,
            bytes_accessed=2 * count * depth * feats,
            transcendentals=0,
        ),
        name="down",
    )(table, *blocks, w_down, *more)


def down_last(table, total, first, second, slot, w_down, j, parts, experts, final):
    half, depth = first.shape
    m = 2 * half
    feats = w_down.shape[0]
    share = m // experts

    def kernel(tab, a_ref, b_ref, w_ref, total_ref, *refs):
        target = refs[-1] if final else refs[0]
        there = pl.ds(pl.multiple_of((tab[slot] * parts + j) * depth, depth), depth)
        target[:half, :] = total_ref[:half, :] + dot_nt(a_ref[...], w_ref[:, there])
        target[half:, :] = total_ref[half:, :] + dot_nt(b_ref[...], w_ref[:, there])
        if final:
            for i in range(experts):
                start = pl.multiple_of((tab[1] ^ i) * share, share)
                refs[i][...] = target[pl.ds(start, share), :].astype(jnp.bfloat16)

    if final:
        out_shape = [jax.ShapeDtypeStruct((share, feats), jnp.bfloat16)] * experts
        out_specs = [WHOLE] * experts
    else:
        out_shape = jax.ShapeDtypeStruct((m, feats), jnp.float32)
        out_specs = WHOLE
    return pl.pallas_call(
        kernel,
        grid_spec=pltpu.PrefetchScalarGridSpec(
            num_scalar_prefetch=1,
            in_specs=[WHOLE] * 4,
            out_specs=out_specs,
            scratch_shapes=[pltpu.VMEM((m, feats), jnp.float32)] if final else [],
        ),
        out_shape=out_shape,
        compiler_params=params(8),
        cost_estimate=pl.CostEstimate(
            flops=2 * m * depth * feats, bytes_accessed=2 * depth * feats, transcendentals=0
        ),
        name="down_last",
    )(table, first, second, w_down, total)


def combine(table, pieces, routing, n, base):
    experts = len(pieces)
    share, feats = pieces[0].shape
    rows = routing.shape[0] // n
    group = share // rows

    def kernel(tab, *refs):
        ins, route_ref, outs, route = refs[:experts], refs[experts], refs[experts + 1 : -1], refs[-1]
        route[...] = route_ref[...].astype(jnp.float32)
        for k in range(group):
            block = lax.rem(k + tab[2], group)
            info = route[pl.ds(pl.multiple_of(tab[base + k] * rows, rows), rows), :]
            unit0 = info[:, 2:3] * 256.0 + info[:, 4:5]
            unit1 = info[:, 3:4] * 256.0 + info[:, 5:6]
            whole = unit0 + unit1
            share0, share1 = unit0 / whole, unit1 / whole
            mixed = jnp.zeros((rows, feats), jnp.float32)
            for i in range(experts):
                name = (tab[1] ^ i).astype(jnp.float32)
                weight = jnp.where(info[:, 0:1] == name, share0, 0.0)
                weight += jnp.where(info[:, 1:2] == name, share1, 0.0)
                mixed += weight * ins[i][block].astype(jnp.float32)
            outs[k][...] = mixed.astype(jnp.bfloat16)

    return pl.pallas_call(
        kernel,
        grid_spec=pltpu.PrefetchScalarGridSpec(
            num_scalar_prefetch=1,
            in_specs=[WHOLE] * (experts + 1),
            out_specs=[WHOLE] * group,
            scratch_shapes=[pltpu.VMEM(routing.shape, jnp.float32)],
        ),
        out_shape=[jax.ShapeDtypeStruct((rows, feats), jnp.bfloat16)] * group,
        compiler_params=params(16),
        name="combine",
    )(table, *[piece.reshape(group, rows, feats) for piece in pieces], routing)


def assemble(table, pieces):
    group = len(pieces)
    rows, feats = pieces[0].shape

    def kernel(tab, *refs):
        out = refs[-1]
        for k in range(group):
            spot = lax.rem(tab[2] - k + group, group)
            for s in range(group):

                @pl.when(spot == s)
                def _():
                    out[:, s * feats : (s + 1) * feats] = refs[k][...]

    return pl.pallas_call(
        kernel,
        grid_spec=pltpu.PrefetchScalarGridSpec(
            num_scalar_prefetch=1, grid=(1,), in_specs=[WHOLE] * group, out_specs=WHOLE
        ),
        out_shape=jax.ShapeDtypeStruct((rows, group * feats), jnp.bfloat16),
        compiler_params=params(16),
        name="assemble",
    )(table, *pieces)


def local(tokens, expert_ids, gate_units, gate_weight, up_weight, down_weight):
    experts = lax.axis_size("expert")
    n = lax.axis_size("tensor")
    group = n // experts
    rows, width = tokens.shape
    w_gate, w_up = (
        pltpu.with_memory_space_constraint(w[0], pltpu.HBM) for w in (gate_weight, up_weight)
    )
    w_down = down_weight[0]
    part = width // 2
    tile = next(k for k in (512, 384, 256, 128) if part % (2 * k) == 0)
    parts = 2 if w_gate.shape[1] % (2 * LANES) == 0 else 1

    me = lax.axis_index(("expert", "tensor")).astype(jnp.uint32)
    rows_of = jnp.asarray(tables(experts, n))
    length = rows_of.shape[1]
    table = lax.dynamic_slice(rows_of, (me, jnp.uint32(0)), (1, length)).reshape(length)

    ring = ring_of(n)
    ahead = [(ring[p], ring[(p + 1) % n]) for p in range(n)]
    behind = [(b, a) for a, b in ahead]

    core = (lax.axis_index("expert") & 1).reshape(1)
    own = prepare(core, tokens, expert_ids.T, gate_units.T)
    brought = [[block] for block in own]
    forward, backward = list(own), list(own)
    cut = part // 2
    near = part // 4 // LANES * LANES
    for hop in range(1, n // 2 + 1):
        for q in range(2):
            if hop < n // 2:
                forward[q] = lax.ppermute(forward[q], "tensor", ahead)
                backward[q] = lax.ppermute(backward[q], "tensor", behind)
                brought[q] += [forward[q], backward[q]]
            else:
                forward[q] = lax.ppermute(forward[q][:, :near], "tensor", ahead)
                backward[q] = lax.ppermute(backward[q][:, near:], "tensor", behind)
    def stacked(blocks, cols):
        whole = jnp.zeros((n * rows, cols.stop - cols.start), tokens.dtype)
        for slot, block in enumerate(blocks):
            whole = lax.dynamic_update_slice(whole, block[:, cols], (slot * rows, 0))
        return whole

    sums, other = [], []
    for q in range(2):
        if q:
            forward[q], backward[q], sums = lax.optimization_barrier((forward[q], backward[q], sums))
        brought[q].append(jnp.concatenate([forward[q], backward[q]], axis=1))
        collected = stacked(brought[q], slice(0, cut))
        other.append(lax.ppermute(collected, "expert", [(i, i ^ 1) for i in range(experts)]))
        sums = depth_part(table, collected, w_gate, w_up, q, sums, tile)
    routing = stacked(brought[1], slice(cut, cut + LANES))

    hidden = [
        hidden_part(table, other, w_gate, w_up, sums, n, j, parts, tile)
        for j in range(parts)
    ]
    total = None
    held = [([block], [3]) for block in hidden]
    half = n * rows // 2
    for hop in range(1, n // 2 + 1):
        came = []
        for j in range(parts):
            blocks, slots = held[j]
            if j == 0 and total is not None:
                blocks, total = lax.optimization_barrier((blocks, total))
            forward, backward = blocks[0], blocks[-1]
            if hop < n // 2:
                forward = lax.ppermute(forward, "tensor", ahead)
                backward = lax.ppermute(backward, "tensor", behind)
                held[j] = ([forward, backward], [2 + 2 * hop, 3 + 2 * hop])
            else:
                forward = lax.ppermute(forward[:half], "tensor", ahead)
                backward = lax.ppermute(backward[half:], "tensor", behind)
                held[j] = (forward, backward)
            came += [(block, (slot, j)) for block, slot in zip(blocks, slots)]
        total = down_step(table, total, [c[0] for c in came], [c[1] for c in came], w_down, parts)
    for j in range(parts):
        total = down_last(
            table, total, *held[j], 2 + n, w_down, j, parts, experts, j == parts - 1
        )

    pieces = [total[0]] + [
        lax.ppermute(total[i], "expert", [(s, s ^ i) for s in range(experts)])
        for i in range(1, experts)
    ]
    mixed = combine(table, pieces, routing, n, 3 + n)
    arrived = []
    for k in range(group):
        pairs = []
        for e in range(experts):
            for t in range(n):
                pairs.append((e * n + t, (t // group) * n + group * e + (k + t) % group))
        arrived.append(lax.ppermute(mixed[k], ("expert", "tensor"), pairs))
    return assemble(table, arrived)


def solution(mesh):
    return jax.shard_map(
        local,
        mesh=mesh,
        in_specs=(
            P("tensor", None),
            P("tensor", None),
            P("tensor", None),
            P("expert", None, "tensor"),
            P("expert", None, "tensor"),
            P("expert", "tensor", None),
        ),
        out_specs=P("tensor", "expert"),
        check_vma=False,
    )
```

```python
import jax
import jax.numpy as jnp
import numpy as np
from jax import lax
from jax.experimental import pallas as pl
from jax.experimental.pallas import tpu as pltpu
from jax.sharding import PartitionSpec as P

LANES = 128
WHOLE = pl.BlockSpec(memory_space=pltpu.VMEM)


def ring_of(count):
    return list(range(0, count, 2)) + list(range(count - 1, 0, -2))


def hop_list(count):
    hops = [0]
    for hop in range(1, count // 2):
        hops += [hop, -hop]
    return hops + [count // 2]


def tables(experts, n):
    ring = ring_of(n)
    hops = hop_list(n)
    group = n // experts
    rows = []
    for e in range(experts):
        for t in range(n):
            place = ring.index(t)
            sources = [ring[(place - hop) % n] for hop in hops]
            mine = [sources.index(group * e + (i + t) % group) for i in range(group)]
            rows.append([e % 2, e, t % group] + sources + mine)
    return np.array(rows, np.int32)


def params(megabytes):
    return pltpu.CompilerParams(vmem_limit_bytes=megabytes << 20)


def dot(a, b):
    return jnp.dot(a, b, preferred_element_type=jnp.float32)


def dot_nt(a, b):
    return lax.dot_general(a, b, (((1,), (1,)), ((), ())), preferred_element_type=jnp.float32)


def prepare(core, tokens, expert_ids, gate_units):
    rows, width = tokens.shape
    part = width // 2
    cut = part // 2

    def kernel(core_ref, tokens_ref, ids_ref, units_ref, low, high, ids, units, sems):
        start = pl.multiple_of(core_ref[0] * part, part)
        copies = [
            pltpu.make_async_copy(source, target, sems.at[i])
            for i, (source, target) in enumerate(
                [
                    (ids_ref, ids),
                    (units_ref, units),
                    (tokens_ref.at[:, pl.ds(start, cut)], low),
                    (tokens_ref.at[:, pl.ds(start + cut, cut)], high.at[:, :cut]),
                ]
            )
        ]
        for copy in copies:
            copy.start()
        copies[0].wait()
        copies[1].wait()
        number = units[...]
        lines = [ids[...], number >> 8, number & 255]
        route = jnp.concatenate(
            [line.astype(jnp.float32) for line in lines] + [jnp.zeros((2, rows), jnp.float32)], axis=0
        )
        route = jnp.concatenate([route, jnp.zeros((8, LANES - rows), jnp.float32)], axis=1)
        route = jnp.concatenate([route, jnp.zeros((LANES - 8, LANES), jnp.float32)], axis=0)
        high[:, cut:] = route.T[:rows, :].astype(jnp.bfloat16)
        copies[2].wait()
        copies[3].wait()

    hbm = pl.BlockSpec(memory_space=pltpu.HBM)
    return pl.pallas_call(
        kernel,
        grid_spec=pltpu.PrefetchScalarGridSpec(
            num_scalar_prefetch=1,
            in_specs=[hbm] * 3,
            out_specs=[WHOLE, WHOLE],
            scratch_shapes=[
                pltpu.VMEM((2, rows), jnp.int32),
                pltpu.VMEM((2, rows), jnp.int32),
                pltpu.SemaphoreType.DMA((4,)),
            ],
        ),
        out_shape=[
            pltpu.VMEM((rows, cut), tokens.dtype),
            pltpu.VMEM((rows, cut + LANES), tokens.dtype),
        ],
        compiler_params=params(4),
        name="prepare",
    )(core, *[pltpu.with_memory_space_constraint(a, pltpu.HBM) for a in (tokens, expert_ids, gate_units)])


def column_tiles(units):
    size = 256 if units % 256 == 0 else units
    return [slice(i, i + size) for i in range(0, units, size)]


def depth_part(table, x, w_gate, w_up, q, sums, tile):
    m, depth = x.shape
    units = w_gate.shape[1]
    steps = depth // tile

    def kernel(tab, x_ref, g_ref, u_ref, *refs):
        gate, up = refs[-2:]

        def add(first):
            for cols in column_tiles(units):
                for w_ref, out, before in ((g_ref, gate, 0), (u_ref, up, 1)):
                    product = dot(x_ref[...], w_ref[:, cols])
                    if not first:
                        product += out[:, cols]
                    elif sums:
                        product += refs[before][:, cols]
                    out[:, cols] = product

        pl.when(pl.program_id(0) == 0)(lambda: add(True))
        pl.when(pl.program_id(0) > 0)(lambda: add(False))

    weight = pl.BlockSpec((tile, units), lambda k, tab: ((2 * tab[0] + q) * steps + k, 0))
    out = jax.ShapeDtypeStruct((m, units), jnp.float32)
    return pl.pallas_call(
        kernel,
        grid_spec=pltpu.PrefetchScalarGridSpec(
            num_scalar_prefetch=1,
            grid=(steps,),
            in_specs=[pl.BlockSpec((m, tile), lambda k, tab: (0, k)), weight, weight]
            + [WHOLE] * len(sums),
            out_specs=[WHOLE, WHOLE],
        ),
        out_shape=[out, out],
        compiler_params=params(16),
        cost_estimate=pl.CostEstimate(
            flops=4 * m * depth * units, bytes_accessed=4 * depth * units, transcendentals=0
        ),
        name="gate_up",
    )(table, x, w_gate, w_up, *sums)


def hidden_part(table, xs, w_gate, w_up, sums, n, j, parts, tile):
    m, depth = xs[0].shape
    units = w_gate.shape[1] // parts
    rows = m // n
    steps = depth // tile

    def kernel(tab, x0, x1, g_ref, u_ref, gate_in, up_in, out, gate, up):
        k = pl.program_id(0)

        def add(x_ref, first):
            for cols in column_tiles(units):
                for w_ref, total, before in ((g_ref, gate, gate_in), (u_ref, up, up_in)):
                    so_far = before if first else total
                    total[:, cols] = so_far[:, cols] + dot(x_ref[...], w_ref[:, cols])

        pl.when(k == 0)(lambda: add(x0, True))
        pl.when((k > 0) & (k < steps))(lambda: add(x0, False))
        pl.when(k >= steps)(lambda: add(x1, False))

        @pl.when(k == 2 * steps - 1)
        def _():
            for r in range(n):
                piece = slice(r * rows, (r + 1) * rows)
                value = gate[piece, :]
                hidden = value * jax.nn.sigmoid(value) * up[piece, :]
                out[tab[3 + r]] = hidden.astype(out.dtype)

    weight = pl.BlockSpec((tile, units), lambda k, tab: (2 * (1 - tab[0]) * steps + k, j))
    part_sum = pl.BlockSpec((m, units), lambda k, tab: (0, j))
    return pl.pallas_call(
        kernel,
        grid_spec=pltpu.PrefetchScalarGridSpec(
            num_scalar_prefetch=1,
            grid=(2 * steps,),
            in_specs=[
                pl.BlockSpec((m, tile), lambda k, tab: (0, jnp.minimum(k, steps - 1))),
                pl.BlockSpec((m, tile), lambda k, tab: (0, jnp.maximum(k - steps, 0))),
                weight,
                weight,
                part_sum,
                part_sum,
            ],
            out_specs=WHOLE,
            scratch_shapes=[pltpu.VMEM((m, units), jnp.float32)] * 2,
        ),
        out_shape=jax.ShapeDtypeStruct((n, rows, units), jnp.bfloat16),
        compiler_params=params(16),
        cost_estimate=pl.CostEstimate(
            flops=8 * m * depth * units, bytes_accessed=8 * depth * units, transcendentals=m * units
        ),
        name="hidden",
    )(table, *xs, w_gate, w_up, *sums).reshape(m, units)


def down_step(table, total, blocks, places, w_down, parts):
    m, depth = blocks[0].shape
    feats = w_down.shape[0]
    count = len(blocks)

    def kernel(tab, *refs):
        lhs, w_ref, out = refs[:count], refs[count], refs[-1]
        for i, (slot, j) in enumerate(places):
            start = pl.multiple_of((tab[slot] * parts + j) * depth, depth)
            product = dot_nt(lhs[i][...], w_ref[:, pl.ds(start, depth)])
            if i:
                out[...] += product
            elif total is None:
                out[...] = product
            else:
                out[...] = refs[count + 1][...] + product

    more = [] if total is None else [total]
    return pl.pallas_call(
        kernel,
        grid_spec=pltpu.PrefetchScalarGridSpec(
            num_scalar_prefetch=1,
            in_specs=[WHOLE] * (count + 1 + len(more)),
            out_specs=WHOLE,
        ),
        out_shape=jax.ShapeDtypeStruct((m, feats), jnp.float32),
        compiler_params=params(8),
        cost_estimate=pl.CostEstimate(
            flops=2 * count * m * depth * feats,
            bytes_accessed=2 * count * depth * feats,
            transcendentals=0,
        ),
        name="down",
    )(table, *blocks, w_down, *more)


def down_last(table, total, first, second, slot, w_down, j, parts, experts, final):
    half, depth = first.shape
    m = 2 * half
    feats = w_down.shape[0]
    share = m // experts

    def kernel(tab, a_ref, b_ref, w_ref, total_ref, *refs):
        target = refs[-1] if final else refs[0]
        there = pl.ds(pl.multiple_of((tab[slot] * parts + j) * depth, depth), depth)
        target[:half, :] = total_ref[:half, :] + dot_nt(a_ref[...], w_ref[:, there])
        target[half:, :] = total_ref[half:, :] + dot_nt(b_ref[...], w_ref[:, there])
        if final:
            for i in range(experts):
                start = pl.multiple_of((tab[1] ^ i) * share, share)
                refs[i][...] = target[pl.ds(start, share), :].astype(jnp.bfloat16)

    if final:
        out_shape = [jax.ShapeDtypeStruct((share, feats), jnp.bfloat16)] * experts
        out_specs = [WHOLE] * experts
    else:
        out_shape = jax.ShapeDtypeStruct((m, feats), jnp.float32)
        out_specs = WHOLE
    return pl.pallas_call(
        kernel,
        grid_spec=pltpu.PrefetchScalarGridSpec(
            num_scalar_prefetch=1,
            in_specs=[WHOLE] * 4,
            out_specs=out_specs,
            scratch_shapes=[pltpu.VMEM((m, feats), jnp.float32)] if final else [],
        ),
        out_shape=out_shape,
        compiler_params=params(8),
        cost_estimate=pl.CostEstimate(
            flops=2 * m * depth * feats, bytes_accessed=2 * depth * feats, transcendentals=0
        ),
        name="down_last",
    )(table, first, second, w_down, total)


def combine(table, pieces, routing, n, base):
    experts = len(pieces)
    share, feats = pieces[0].shape
    rows = routing.shape[0] // n
    group = share // rows

    def kernel(tab, *refs):
        ins, route_ref, outs, route = refs[:experts], refs[experts], refs[experts + 1 : -1], refs[-1]
        route[...] = route_ref[...].astype(jnp.float32)
        for k in range(group):
            block = lax.rem(k + tab[2], group)
            info = route[pl.ds(pl.multiple_of(tab[base + k] * rows, rows), rows), :]
            unit0 = info[:, 2:3] * 256.0 + info[:, 4:5]
            unit1 = info[:, 3:4] * 256.0 + info[:, 5:6]
            whole = unit0 + unit1
            share0, share1 = unit0 / whole, unit1 / whole
            mixed = jnp.zeros((rows, feats), jnp.float32)
            for i in range(experts):
                name = (tab[1] ^ i).astype(jnp.float32)
                weight = jnp.where(info[:, 0:1] == name, share0, 0.0)
                weight += jnp.where(info[:, 1:2] == name, share1, 0.0)
                mixed += weight * ins[i][block].astype(jnp.float32)
            outs[k][...] = mixed.astype(jnp.bfloat16)

    return pl.pallas_call(
        kernel,
        grid_spec=pltpu.PrefetchScalarGridSpec(
            num_scalar_prefetch=1,
            in_specs=[WHOLE] * (experts + 1),
            out_specs=[WHOLE] * group,
            scratch_shapes=[pltpu.VMEM(routing.shape, jnp.float32)],
        ),
        out_shape=[jax.ShapeDtypeStruct((rows, feats), jnp.bfloat16)] * group,
        compiler_params=params(16),
        name="combine",
    )(table, *[piece.reshape(group, rows, feats) for piece in pieces], routing)


def assemble(table, pieces):
    group = len(pieces)
    rows, feats = pieces[0].shape

    def kernel(tab, *refs):
        out = refs[-1]
        for k in range(group):
            spot = lax.rem(tab[2] - k + group, group)
            for s in range(group):

                @pl.when(spot == s)
                def _():
                    out[:, s * feats : (s + 1) * feats] = refs[k][...]

    return pl.pallas_call(
        kernel,
        grid_spec=pltpu.PrefetchScalarGridSpec(
            num_scalar_prefetch=1, grid=(1,), in_specs=[WHOLE] * group, out_specs=WHOLE
        ),
        out_shape=jax.ShapeDtypeStruct((rows, group * feats), jnp.bfloat16),
        compiler_params=params(16),
        name="assemble",
    )(table, *pieces)


def local(tokens, expert_ids, gate_units, gate_weight, up_weight, down_weight):
    experts = lax.axis_size("expert")
    n = lax.axis_size("tensor")
    group = n // experts
    rows, width = tokens.shape
    w_gate, w_up = (
        pltpu.with_memory_space_constraint(w[0], pltpu.HBM) for w in (gate_weight, up_weight)
    )
    w_down = down_weight[0]
    part = width // 2
    tile = next(k for k in (512, 384, 256, 128) if part % (2 * k) == 0)
    parts = 2 if w_gate.shape[1] % (2 * LANES) == 0 else 1

    me = lax.axis_index(("expert", "tensor")).astype(jnp.uint32)
    rows_of = jnp.asarray(tables(experts, n))
    length = rows_of.shape[1]
    table = lax.dynamic_slice(rows_of, (me, jnp.uint32(0)), (1, length)).reshape(length)

    ring = ring_of(n)
    ahead = [(ring[p], ring[(p + 1) % n]) for p in range(n)]
    behind = [(b, a) for a, b in ahead]

    core = (lax.axis_index("expert") & 1).reshape(1)
    own = prepare(core, tokens, expert_ids.T, gate_units.T)
    brought = [[block] for block in own]
    forward, backward = list(own), list(own)
    cut = part // 2
    near = part // 4 // LANES * LANES
    for hop in range(1, n // 2 + 1):
        for q in range(2):
            if hop < n // 2:
                forward[q] = lax.ppermute(forward[q], "tensor", ahead)
                backward[q] = lax.ppermute(backward[q], "tensor", behind)
                brought[q] += [forward[q], backward[q]]
            else:
                forward[q] = lax.ppermute(forward[q][:, :near], "tensor", ahead)
                backward[q] = lax.ppermute(backward[q][:, near:], "tensor", behind)
    def stacked(blocks, cols):
        whole = jnp.zeros((n * rows, cols.stop - cols.start), tokens.dtype)
        for slot, block in enumerate(blocks):
            whole = lax.dynamic_update_slice(whole, block[:, cols], (slot * rows, 0))
        return whole

    sums, other = [], []
    for q in range(2):
        if q:
            forward[q], backward[q], sums = lax.optimization_barrier((forward[q], backward[q], sums))
        brought[q].append(jnp.concatenate([forward[q], backward[q]], axis=1))
        collected = stacked(brought[q], slice(0, cut))
        other.append(lax.ppermute(collected, "expert", [(i, i ^ 1) for i in range(experts)]))
        sums = depth_part(table, collected, w_gate, w_up, q, sums, tile)
    routing = stacked(brought[1], slice(cut, cut + LANES))

    hidden = [
        hidden_part(table, other, w_gate, w_up, sums, n, j, parts, tile)
        for j in range(parts)
    ]
    total = None
    held = [([block], [3]) for block in hidden]
    half = n * rows // 2
    for hop in range(1, n // 2 + 1):
        came = []
        for j in range(parts):
            blocks, slots = held[j]
            if j == 0 and total is not None:
                blocks, total = lax.optimization_barrier((blocks, total))
            forward, backward = blocks[0], blocks[-1]
            if hop < n // 2:
                forward = lax.ppermute(forward, "tensor", ahead)
                backward = lax.ppermute(backward, "tensor", behind)
                held[j] = ([forward, backward], [2 + 2 * hop, 3 + 2 * hop])
            else:
                forward = lax.ppermute(forward[:half], "tensor", ahead)
                backward = lax.ppermute(backward[half:], "tensor", behind)
                held[j] = (forward, backward)
            came += [(block, (slot, j)) for block, slot in zip(blocks, slots)]
        total = down_step(table, total, [c[0] for c in came], [c[1] for c in came], w_down, parts)
    for j in range(parts):
        total = down_last(
            table, total, *held[j], 2 + n, w_down, j, parts, experts, j == parts - 1
        )

    pieces = [total[0]] + [
        lax.ppermute(total[i], "expert", [(s, s ^ i) for s in range(experts)])
        for i in range(1, experts)
    ]
    mixed = combine(table, pieces, routing, n, 3 + n)
    arrived = []
    for k in range(group):
        pairs = []
        for e in range(experts):
            for t in range(n):
                pairs.append((e * n + t, (t // group) * n + group * e + (k + t) % group))
        arrived.append(lax.ppermute(mixed[k], ("expert", "tensor"), pairs))
    return assemble(table, arrived)


def solution(mesh):
    return jax.shard_map(
        local,
        mesh=mesh,
        in_specs=(
            P("tensor", None),
            P("tensor", None),
            P("tensor", None),
            P("expert", None, "tensor"),
            P("expert", None, "tensor"),
            P("expert", "tensor", None),
        ),
        out_specs=P("tensor", "expert"),
        check_vma=False,
    )
```

```python
import jax
import jax.numpy as jnp
import numpy as np
from jax import lax
from jax.experimental import pallas as pl
from jax.experimental.pallas import tpu as pltpu
from jax.sharding import PartitionSpec as P

LANES = 128
WHOLE = pl.BlockSpec(memory_space=pltpu.VMEM)


def ring_of(count):
    return list(range(0, count, 2)) + list(range(count - 1, 0, -2))


def hop_list(count):
    hops = [0]
    for hop in range(1, count // 2):
        hops += [hop, -hop]
    return hops + [count // 2]


def tables(experts, n):
    ring = ring_of(n)
    hops = hop_list(n)
    group = n // experts
    rows = []
    for e in range(experts):
        for t in range(n):
            place = ring.index(t)
            sources = [ring[(place - hop) % n] for hop in hops]
            mine = [sources.index(group * e + (i + t) % group) for i in range(group)]
            rows.append([e % 2, e, t % group] + sources + mine)
    return np.array(rows, np.int32)


def params(megabytes):
    return pltpu.CompilerParams(vmem_limit_bytes=megabytes << 20)


def dot(a, b):
    return jnp.dot(a, b, preferred_element_type=jnp.float32)


def dot_nt(a, b):
    return lax.dot_general(a, b, (((1,), (1,)), ((), ())), preferred_element_type=jnp.float32)


def prepare(core, tokens, expert_ids, gate_units, meanwhile):
    rows, width = tokens.shape
    part = width // 2
    cut = part // 2

    def kernel(core_ref, tokens_ref, ids_ref, units_ref, low, high, ids, units, sems):
        start = pl.multiple_of(core_ref[0] * part, part)
        copies = [
            pltpu.make_async_copy(source, target, sems.at[i])
            for i, (source, target) in enumerate(
                [
                    (ids_ref, ids),
                    (units_ref, units),
                    (tokens_ref.at[:, pl.ds(start, cut)], low),
                    (tokens_ref.at[:, pl.ds(start + cut, cut)], high.at[:, :cut]),
                ]
            )
        ]
        for copy in copies:
            copy.start()
        copies[0].wait()
        copies[1].wait()
        number = units[...]
        lines = [ids[...], number >> 8, number & 255]
        route = jnp.concatenate(
            [line.astype(jnp.float32) for line in lines] + [jnp.zeros((2, rows), jnp.float32)], axis=0
        )
        route = jnp.concatenate([route, jnp.zeros((8, LANES - rows), jnp.float32)], axis=1)
        route = jnp.concatenate([route, jnp.zeros((LANES - 8, LANES), jnp.float32)], axis=0)
        high[:, cut:] = route.T[:rows, :].astype(jnp.bfloat16)
        copies[2].wait()
        copies[3].wait()

    hbm = pl.BlockSpec(memory_space=pltpu.HBM)
    return pl.pallas_call(
        kernel,
        grid_spec=pltpu.PrefetchScalarGridSpec(
            num_scalar_prefetch=1,
            in_specs=[hbm] * 3,
            out_specs=[WHOLE, WHOLE],
            scratch_shapes=[
                pltpu.VMEM((2, rows), jnp.int32),
                pltpu.VMEM((2, rows), jnp.int32),
                pltpu.SemaphoreType.DMA((4,)),
            ],
        ),
        out_shape=[
            pltpu.VMEM((rows, cut), tokens.dtype),
            pltpu.VMEM((rows, cut + LANES), tokens.dtype),
        ],
        compiler_params=params(4),
        cost_estimate=pl.CostEstimate(flops=meanwhile, bytes_accessed=0, transcendentals=0),
        name="prepare",
    )(core, *[pltpu.with_memory_space_constraint(a, pltpu.HBM) for a in (tokens, expert_ids, gate_units)])


def column_tiles(units):
    size = 256 if units % 256 == 0 else units
    return [slice(i, i + size) for i in range(0, units, size)]


def depth_part(table, x, w_gate, w_up, other, q, sums):
    m, depth = x.shape
    units = w_gate.shape[1]

    def kernel(tab, x_ref, g_ref, u_ref, *refs):
        gate, up = refs[-2:]
        side = 1 - tab[0] if other else tab[0]
        rows = pl.ds(pl.multiple_of((2 * side + q) * depth, depth), depth)
        for cols in column_tiles(units):
            for w_ref, out, before in ((g_ref, gate, 0), (u_ref, up, 1)):
                product = dot(x_ref[...], w_ref[rows, cols])
                if sums:
                    product += refs[before][:, cols]
                out[:, cols] = product

    out = jax.ShapeDtypeStruct((m, units), jnp.float32)
    return pl.pallas_call(
        kernel,
        grid_spec=pltpu.PrefetchScalarGridSpec(
            num_scalar_prefetch=1,
            in_specs=[WHOLE] * (3 + len(sums)),
            out_specs=[WHOLE, WHOLE],
        ),
        out_shape=[out, out],
        compiler_params=params(8),
        cost_estimate=pl.CostEstimate(
            flops=4 * m * depth * units, bytes_accessed=4 * depth * units, transcendentals=0
        ),
        name="gate_up",
    )(table, x, w_gate, w_up, *sums)


def hidden_part(table, x, w_gate, w_up, q, sums, n, j, parts):
    m, depth = x.shape
    units = w_gate.shape[1] // parts
    rows = m // n

    def kernel(tab, x_ref, g_ref, u_ref, gate_ref, up_ref, out):
        deep = pl.ds(pl.multiple_of((2 * (1 - tab[0]) + q) * depth, depth), depth)
        for cols in column_tiles(units):
            there = slice(j * units + cols.start, j * units + cols.stop)
            gate = gate_ref[:, there] + dot(x_ref[...], g_ref[deep, there])
            up = up_ref[:, there] + dot(x_ref[...], u_ref[deep, there])
            hidden = (gate * jax.nn.sigmoid(gate) * up).astype(out.dtype)
            for r in range(n):
                out[tab[3 + r], :, cols] = hidden[r * rows : (r + 1) * rows, :]

    return pl.pallas_call(
        kernel,
        grid_spec=pltpu.PrefetchScalarGridSpec(
            num_scalar_prefetch=1, in_specs=[WHOLE] * 5, out_specs=WHOLE
        ),
        out_shape=jax.ShapeDtypeStruct((n, rows, units), jnp.bfloat16),
        compiler_params=params(8),
        cost_estimate=pl.CostEstimate(
            flops=4 * m * depth * units, bytes_accessed=4 * depth * units, transcendentals=m * units
        ),
        name="hidden",
    )(table, x, w_gate, w_up, *sums).reshape(m, units)


def down_step(table, total, blocks, places, w_down, parts):
    m, depth = blocks[0].shape
    feats = w_down.shape[0]
    count = len(blocks)

    def kernel(tab, *refs):
        lhs, w_ref, out = refs[:count], refs[count], refs[-1]
        for i, (slot, j) in enumerate(places):
            start = pl.multiple_of((tab[slot] * parts + j) * depth, depth)
            product = dot_nt(lhs[i][...], w_ref[:, pl.ds(start, depth)])
            if i:
                out[...] += product
            elif total is None:
                out[...] = product
            else:
                out[...] = refs[count + 1][...] + product

    more = [] if total is None else [total]
    return pl.pallas_call(
        kernel,
        grid_spec=pltpu.PrefetchScalarGridSpec(
            num_scalar_prefetch=1,
            in_specs=[WHOLE] * (count + 1 + len(more)),
            out_specs=WHOLE,
        ),
        out_shape=jax.ShapeDtypeStruct((m, feats), jnp.float32),
        compiler_params=params(8),
        cost_estimate=pl.CostEstimate(
            flops=2 * count * m * depth * feats,
            bytes_accessed=2 * count * depth * feats,
            transcendentals=0,
        ),
        name="down",
    )(table, *blocks, w_down, *more)


def down_last(table, total, first, second, slot, w_down, j, parts, experts, final):
    half, depth = first.shape
    m = 2 * half
    feats = w_down.shape[0]
    share = m // experts

    def kernel(tab, a_ref, b_ref, w_ref, total_ref, *refs):
        target = refs[-1] if final else refs[0]
        there = pl.ds(pl.multiple_of((tab[slot] * parts + j) * depth, depth), depth)
        target[:half, :] = total_ref[:half, :] + dot_nt(a_ref[...], w_ref[:, there])
        target[half:, :] = total_ref[half:, :] + dot_nt(b_ref[...], w_ref[:, there])
        if final:
            for i in range(experts):
                start = pl.multiple_of((tab[1] ^ i) * share, share)
                refs[i][...] = target[pl.ds(start, share), :].astype(jnp.bfloat16)

    if final:
        out_shape = [jax.ShapeDtypeStruct((share, feats), jnp.bfloat16)] * experts
        out_specs = [WHOLE] * experts
    else:
        out_shape = jax.ShapeDtypeStruct((m, feats), jnp.float32)
        out_specs = WHOLE
    return pl.pallas_call(
        kernel,
        grid_spec=pltpu.PrefetchScalarGridSpec(
            num_scalar_prefetch=1,
            in_specs=[WHOLE] * 4,
            out_specs=out_specs,
            scratch_shapes=[pltpu.VMEM((m, feats), jnp.float32)] if final else [],
        ),
        out_shape=out_shape,
        compiler_params=params(8),
        cost_estimate=pl.CostEstimate(
            flops=2 * m * depth * feats, bytes_accessed=2 * depth * feats, transcendentals=0
        ),
        name="down_last",
    )(table, first, second, w_down, total)


def combine(table, pieces, routing, n, base):
    experts = len(pieces)
    share, feats = pieces[0].shape
    rows = routing.shape[0] // n
    group = share // rows

    def kernel(tab, *refs):
        ins, route_ref, outs, route = refs[:experts], refs[experts], refs[experts + 1 : -1], refs[-1]
        route[...] = route_ref[...].astype(jnp.float32)
        for k in range(group):
            block = lax.rem(k + tab[2], group)
            info = route[pl.ds(pl.multiple_of(tab[base + k] * rows, rows), rows), :]
            unit0 = info[:, 2:3] * 256.0 + info[:, 4:5]
            unit1 = info[:, 3:4] * 256.0 + info[:, 5:6]
            whole = unit0 + unit1
            share0, share1 = unit0 / whole, unit1 / whole
            mixed = jnp.zeros((rows, feats), jnp.float32)
            for i in range(experts):
                name = (tab[1] ^ i).astype(jnp.float32)
                weight = jnp.where(info[:, 0:1] == name, share0, 0.0)
                weight += jnp.where(info[:, 1:2] == name, share1, 0.0)
                mixed += weight * ins[i][block].astype(jnp.float32)
            outs[k][...] = mixed.astype(jnp.bfloat16)

    return pl.pallas_call(
        kernel,
        grid_spec=pltpu.PrefetchScalarGridSpec(
            num_scalar_prefetch=1,
            in_specs=[WHOLE] * (experts + 1),
            out_specs=[WHOLE] * group,
            scratch_shapes=[pltpu.VMEM(routing.shape, jnp.float32)],
        ),
        out_shape=[jax.ShapeDtypeStruct((rows, feats), jnp.bfloat16)] * group,
        compiler_params=params(16),
        name="combine",
    )(table, *[piece.reshape(group, rows, feats) for piece in pieces], routing)


def assemble(table, pieces):
    group = len(pieces)
    rows, feats = pieces[0].shape

    def kernel(tab, *refs):
        out = refs[-1]
        for k in range(group):
            spot = lax.rem(tab[2] - k + group, group)
            for s in range(group):

                @pl.when(spot == s)
                def _():
                    out[:, s * feats : (s + 1) * feats] = refs[k][...]

    return pl.pallas_call(
        kernel,
        grid_spec=pltpu.PrefetchScalarGridSpec(
            num_scalar_prefetch=1, grid=(1,), in_specs=[WHOLE] * group, out_specs=WHOLE
        ),
        out_shape=jax.ShapeDtypeStruct((rows, group * feats), jnp.bfloat16),
        compiler_params=params(16),
        name="assemble",
    )(table, *pieces)


def local(tokens, expert_ids, gate_units, gate_weight, up_weight, down_weight):
    experts = lax.axis_size("expert")
    n = lax.axis_size("tensor")
    group = n // experts
    rows, width = tokens.shape
    w_gate, w_up, w_down = gate_weight[0], up_weight[0], down_weight[0]
    part = width // 2
    parts = 2 if w_gate.shape[1] % (2 * LANES) == 0 else 1

    me = lax.axis_index(("expert", "tensor")).astype(jnp.uint32)
    rows_of = jnp.asarray(tables(experts, n))
    length = rows_of.shape[1]
    table = lax.dynamic_slice(rows_of, (me, jnp.uint32(0)), (1, length)).reshape(length)

    ring = ring_of(n)
    ahead = [(ring[p], ring[(p + 1) % n]) for p in range(n)]
    behind = [(b, a) for a, b in ahead]

    core = (lax.axis_index("expert") & 1).reshape(1)
    meanwhile = 4800 * (w_gate.size + w_up.size)
    own = prepare(core, tokens, expert_ids.T, gate_units.T, meanwhile)
    brought = [[block] for block in own]
    forward, backward = list(own), list(own)
    cut = part // 2
    near = part // 4 // LANES * LANES
    for hop in range(1, n // 2 + 1):
        for q in range(2):
            if hop < n // 2:
                forward[q] = lax.ppermute(forward[q], "tensor", ahead)
                backward[q] = lax.ppermute(backward[q], "tensor", behind)
                brought[q] += [forward[q], backward[q]]
            else:
                forward[q] = lax.ppermute(forward[q][:, :near], "tensor", ahead)
                backward[q] = lax.ppermute(backward[q][:, near:], "tensor", behind)
    def stacked(blocks, cols):
        whole = jnp.zeros((n * rows, cols.stop - cols.start), tokens.dtype)
        for slot, block in enumerate(blocks):
            whole = lax.dynamic_update_slice(whole, block[:, cols], (slot * rows, 0))
        return whole

    sums, other = [], []
    for q in range(2):
        if q:
            forward[q], backward[q], sums = lax.optimization_barrier((forward[q], backward[q], sums))
        brought[q].append(jnp.concatenate([forward[q], backward[q]], axis=1))
        collected = stacked(brought[q], slice(0, cut))
        other.append(lax.ppermute(collected, "expert", [(i, i ^ 1) for i in range(experts)]))
        sums = depth_part(table, collected, w_gate, w_up, False, q, sums)
    sums = depth_part(table, other[0], w_gate, w_up, True, 0, sums)
    routing = stacked(brought[1], slice(cut, cut + LANES))

    hidden = [
        hidden_part(table, other[1], w_gate, w_up, 1, sums, n, j, parts)
        for j in range(parts)
    ]
    total = None
    held = [([block], [3]) for block in hidden]
    half = n * rows // 2
    for hop in range(1, n // 2 + 1):
        came = []
        for j in range(parts):
            blocks, slots = held[j]
            if j == 0 and total is not None:
                blocks, total = lax.optimization_barrier((blocks, total))
            forward, backward = blocks[0], blocks[-1]
            if hop < n // 2:
                forward = lax.ppermute(forward, "tensor", ahead)
                backward = lax.ppermute(backward, "tensor", behind)
                held[j] = ([forward, backward], [2 + 2 * hop, 3 + 2 * hop])
            else:
                forward = lax.ppermute(forward[:half], "tensor", ahead)
                backward = lax.ppermute(backward[half:], "tensor", behind)
                held[j] = (forward, backward)
            came += [(block, (slot, j)) for block, slot in zip(blocks, slots)]
        total = down_step(table, total, [c[0] for c in came], [c[1] for c in came], w_down, parts)
    for j in range(parts):
        total = down_last(
            table, total, *held[j], 2 + n, w_down, j, parts, experts, j == parts - 1
        )

    pieces = [total[0]] + [
        lax.ppermute(total[i], "expert", [(s, s ^ i) for s in range(experts)])
        for i in range(1, experts)
    ]
    mixed = combine(table, pieces, routing, n, 3 + n)
    arrived = []
    for k in range(group):
        pairs = []
        for e in range(experts):
            for t in range(n):
                pairs.append((e * n + t, (t // group) * n + group * e + (k + t) % group))
        arrived.append(lax.ppermute(mixed[k], ("expert", "tensor"), pairs))
    return assemble(table, arrived)


def solution(mesh):
    return jax.shard_map(
        local,
        mesh=mesh,
        in_specs=(
            P("tensor", None),
            P("tensor", None),
            P("tensor", None),
            P("expert", None, "tensor"),
            P("expert", None, "tensor"),
            P("expert", "tensor", None),
        ),
        out_specs=P("tensor", "expert"),
        check_vma=False,
    )
```

```python
import jax
import jax.numpy as jnp
import numpy as np
from jax import lax
from jax.experimental import pallas as pl
from jax.experimental.pallas import tpu as pltpu
from jax.sharding import PartitionSpec as P

LANES = 128
WHOLE = pl.BlockSpec(memory_space=pltpu.VMEM)


def ring_of(count):
    return list(range(0, count, 2)) + list(range(count - 1, 0, -2))


def hop_list(count):
    hops = [0]
    for hop in range(1, count // 2):
        hops += [hop, -hop]
    return hops + [count // 2]


def tables(experts, n):
    ring = ring_of(n)
    hops = hop_list(n)
    group = n // experts
    rows = []
    for e in range(experts):
        for t in range(n):
            place = ring.index(t)
            sources = [ring[(place - hop) % n] for hop in hops]
            mine = [sources.index(group * e + (i + t) % group) for i in range(group)]
            rows.append([e % 2, e, t % group] + sources + mine)
    return np.array(rows, np.int32)


def params(megabytes):
    return pltpu.CompilerParams(vmem_limit_bytes=megabytes << 20)


def dot(a, b):
    return jnp.dot(a, b, preferred_element_type=jnp.float32)


def dot_nt(a, b):
    return lax.dot_general(a, b, (((1,), (1,)), ((), ())), preferred_element_type=jnp.float32)


def prepare(core, tokens, expert_ids, gate_units):
    rows, width = tokens.shape
    part = width // 2

    def kernel(core_ref, tokens_ref, ids_ref, units_ref, out, ids, units, sems):
        start = pl.multiple_of(core_ref[0] * part, part)
        copies = [
            pltpu.make_async_copy(source, target, sems.at[i])
            for i, (source, target) in enumerate(
                [
                    (ids_ref, ids),
                    (units_ref, units),
                    (tokens_ref.at[:, pl.ds(start, part)], out.at[:, :part]),
                ]
            )
        ]
        for copy in copies:
            copy.start()
        copies[0].wait()
        copies[1].wait()
        number = units[...]
        lines = [ids[...], number >> 8, number & 255]
        route = jnp.concatenate(
            [line.astype(jnp.float32) for line in lines] + [jnp.zeros((2, rows), jnp.float32)], axis=0
        )
        route = jnp.concatenate([route, jnp.zeros((8, LANES - rows), jnp.float32)], axis=1)
        route = jnp.concatenate([route, jnp.zeros((LANES - 8, LANES), jnp.float32)], axis=0)
        out[:, part:] = route.T[:rows, :].astype(jnp.bfloat16)
        copies[2].wait()

    hbm = pl.BlockSpec(memory_space=pltpu.HBM)
    return pl.pallas_call(
        kernel,
        grid_spec=pltpu.PrefetchScalarGridSpec(
            num_scalar_prefetch=1,
            in_specs=[hbm] * 3,
            out_specs=WHOLE,
            scratch_shapes=[
                pltpu.VMEM((2, rows), jnp.int32),
                pltpu.VMEM((2, rows), jnp.int32),
                pltpu.SemaphoreType.DMA((3,)),
            ],
        ),
        out_shape=pltpu.VMEM((rows, part + LANES), tokens.dtype),
        compiler_params=params(4),
        name="prepare",
    )(core, *[pltpu.with_memory_space_constraint(a, pltpu.HBM) for a in (tokens, expert_ids, gate_units)])


def bring(w_ref, out, sems, rows, columns):
    pieces = sems.shape[0]
    step = out.shape[0] // pieces
    copies = []
    for i in range(pieces):
        start = rows + i * step
        if not isinstance(start, int):
            start = pl.multiple_of(start, step)
        copies.append(
            pltpu.make_async_copy(
                w_ref.at[pl.ds(start, step), columns], out.at[pl.ds(i * step, step), :], sems.at[i]
            )
        )
    for copy in copies:
        copy.start()
    for copy in copies:
        copy.wait()


def fetch(table, weight, shape, place, after):
    pieces = next(k for k in (8, 4, 2, 1) if shape[0] % (k * 16) == 0)

    def kernel(tab, w_ref, after_ref, out, sems):
        del after_ref
        bring(w_ref, out, sems, *place(tab))

    return pl.pallas_call(
        kernel,
        grid_spec=pltpu.PrefetchScalarGridSpec(
            num_scalar_prefetch=1,
            in_specs=[
                pl.BlockSpec(memory_space=pltpu.HBM),
                pl.BlockSpec(memory_space=pl.ANY),
            ],
            out_specs=WHOLE,
            scratch_shapes=[pltpu.SemaphoreType.DMA((pieces,))],
        ),
        out_shape=pltpu.VMEM(shape, weight.dtype),
        compiler_params=params(4),
        cost_estimate=pl.CostEstimate(
            flops=0, bytes_accessed=4 * shape[0] * shape[1], transcendentals=0
        ),
        name="fetch",
    )(table, weight, after)


def column_tiles(units):
    size = 256 if units % 256 == 0 else units
    return [slice(i, i + size) for i in range(0, units, size)]


def depth_part(x, w_gate, w_up, q, sums):
    m, depth = x.shape
    units = w_gate.shape[1]
    rows = slice(q * depth, (q + 1) * depth)

    def kernel(x_ref, g_ref, u_ref, *refs):
        gate, up = refs[-2:]
        for cols in column_tiles(units):
            for w_ref, out, before in ((g_ref, gate, 0), (u_ref, up, 1)):
                product = dot(x_ref[...], w_ref[rows, cols])
                if sums:
                    product += refs[before][:, cols]
                out[:, cols] = product

    out = jax.ShapeDtypeStruct((m, units), jnp.float32)
    return pl.pallas_call(
        kernel,
        in_specs=[WHOLE] * (3 + len(sums)),
        out_specs=[WHOLE, WHOLE],
        out_shape=[out, out],
        compiler_params=params(8),
        cost_estimate=pl.CostEstimate(
            flops=4 * m * depth * units, bytes_accessed=4 * depth * units, transcendentals=0
        ),
        name="gate_up",
    )(x, w_gate, w_up, *sums)


def hidden_part(table, x, w_gate, w_up, q, sums, n, j, parts):
    m, depth = x.shape
    units = w_gate.shape[1] // parts
    rows = m // n
    deep = slice(q * depth, (q + 1) * depth)

    def kernel(tab, x_ref, g_ref, u_ref, gate_ref, up_ref, out):
        for cols in column_tiles(units):
            there = slice(j * units + cols.start, j * units + cols.stop)
            gate = gate_ref[:, there] + dot(x_ref[...], g_ref[deep, there])
            up = up_ref[:, there] + dot(x_ref[...], u_ref[deep, there])
            hidden = (gate * jax.nn.sigmoid(gate) * up).astype(out.dtype)
            for r in range(n):
                out[tab[3 + r], :, cols] = hidden[r * rows : (r + 1) * rows, :]

    return pl.pallas_call(
        kernel,
        grid_spec=pltpu.PrefetchScalarGridSpec(
            num_scalar_prefetch=1, in_specs=[WHOLE] * 5, out_specs=WHOLE
        ),
        out_shape=jax.ShapeDtypeStruct((n, rows, units), jnp.bfloat16),
        compiler_params=params(12),
        cost_estimate=pl.CostEstimate(
            flops=4 * m * depth * units, bytes_accessed=4 * depth * units, transcendentals=m * units
        ),
        name="hidden",
    )(table, x, w_gate, w_up, *sums).reshape(m, units)


def down_step(table, total, blocks, places, w_down, parts):
    m, depth = blocks[0].shape
    feats = w_down.shape[0]
    count = len(blocks)

    def kernel(tab, *refs):
        lhs, w_ref, out = refs[:count], refs[count], refs[-1]
        for i, (slot, j) in enumerate(places):
            start = pl.multiple_of((tab[slot] * parts + j) * depth, depth)
            product = dot_nt(lhs[i][...], w_ref[:, pl.ds(start, depth)])
            if i:
                out[...] += product
            elif total is None:
                out[...] = product
            else:
                out[...] = refs[count + 1][...] + product

    more = [] if total is None else [total]
    return pl.pallas_call(
        kernel,
        grid_spec=pltpu.PrefetchScalarGridSpec(
            num_scalar_prefetch=1,
            in_specs=[WHOLE] * (count + 1 + len(more)),
            out_specs=WHOLE,
        ),
        out_shape=jax.ShapeDtypeStruct((m, feats), jnp.float32),
        compiler_params=params(8),
        cost_estimate=pl.CostEstimate(
            flops=count * m * depth, bytes_accessed=0, transcendentals=0
        ),
        name="down",
    )(table, *blocks, w_down, *more)


def down_last(table, total, first, second, slot, w_down, j, parts, experts, final):
    half, depth = first.shape
    m = 2 * half
    feats = w_down.shape[0]
    share = m // experts

    def kernel(tab, a_ref, b_ref, w_ref, total_ref, *refs):
        target = refs[-1] if final else refs[0]
        there = pl.ds(pl.multiple_of((tab[slot] * parts + j) * depth, depth), depth)
        target[:half, :] = total_ref[:half, :] + dot_nt(a_ref[...], w_ref[:, there])
        target[half:, :] = total_ref[half:, :] + dot_nt(b_ref[...], w_ref[:, there])
        if final:
            for i in range(experts):
                start = pl.multiple_of((tab[1] ^ i) * share, share)
                refs[i][...] = target[pl.ds(start, share), :].astype(jnp.bfloat16)

    if final:
        out_shape = [jax.ShapeDtypeStruct((share, feats), jnp.bfloat16)] * experts
        out_specs = [WHOLE] * experts
    else:
        out_shape = jax.ShapeDtypeStruct((m, feats), jnp.float32)
        out_specs = WHOLE
    return pl.pallas_call(
        kernel,
        grid_spec=pltpu.PrefetchScalarGridSpec(
            num_scalar_prefetch=1,
            in_specs=[WHOLE] * 4,
            out_specs=out_specs,
            scratch_shapes=[pltpu.VMEM((m, feats), jnp.float32)] if final else [],
        ),
        out_shape=out_shape,
        compiler_params=params(8),
        cost_estimate=pl.CostEstimate(
            flops=m * depth, bytes_accessed=0, transcendentals=0
        ),
        name="down_last",
    )(table, first, second, w_down, total)


def combine(table, pieces, routing, n, base):
    experts = len(pieces)
    share, feats = pieces[0].shape
    rows = routing.shape[0] // n
    group = share // rows

    def kernel(tab, *refs):
        ins, route_ref, (out, route) = refs[:experts], refs[experts], refs[-2:]
        route[...] = route_ref[...].astype(jnp.float32)
        for k in range(group):
            block = lax.rem(k + tab[2], group)
            info = route[pl.ds(pl.multiple_of(tab[base + k] * rows, rows), rows), :]
            unit0 = info[:, 2:3] * 256.0 + info[:, 4:5]
            unit1 = info[:, 3:4] * 256.0 + info[:, 5:6]
            whole = unit0 + unit1
            share0, share1 = unit0 / whole, unit1 / whole
            mixed = jnp.zeros((rows, feats), jnp.float32)
            for i in range(experts):
                name = (tab[1] ^ i).astype(jnp.float32)
                weight = jnp.where(info[:, 0:1] == name, share0, 0.0)
                weight += jnp.where(info[:, 1:2] == name, share1, 0.0)
                mixed += weight * ins[i][block].astype(jnp.float32)
            out[k] = mixed.astype(jnp.bfloat16)

    return pl.pallas_call(
        kernel,
        grid_spec=pltpu.PrefetchScalarGridSpec(
            num_scalar_prefetch=1,
            in_specs=[WHOLE] * (experts + 1),
            out_specs=WHOLE,
            scratch_shapes=[pltpu.VMEM(routing.shape, jnp.float32)],
        ),
        out_shape=jax.ShapeDtypeStruct((group, rows, feats), jnp.bfloat16),
        compiler_params=params(16),
        name="combine",
    )(table, *[piece.reshape(group, rows, feats) for piece in pieces], routing)


def assemble(table, pieces):
    group = len(pieces)
    rows, feats = pieces[0].shape

    def kernel(tab, *refs):
        out = refs[-1]
        for k in range(group):
            spot = lax.rem(tab[2] - k + group, group)
            for s in range(group):

                @pl.when(spot == s)
                def _():
                    out[:, s * feats : (s + 1) * feats] = refs[k][...]

    return pl.pallas_call(
        kernel,
        grid_spec=pltpu.PrefetchScalarGridSpec(
            num_scalar_prefetch=1, grid=(1,), in_specs=[WHOLE] * group, out_specs=WHOLE
        ),
        out_shape=jax.ShapeDtypeStruct((rows, group * feats), jnp.bfloat16),
        compiler_params=params(16),
        name="assemble",
    )(table, *pieces)


def local(tokens, expert_ids, gate_units, gate_weight, up_weight, down_weight):
    experts = lax.axis_size("expert")
    n = lax.axis_size("tensor")
    group = n // experts
    rows, width = tokens.shape
    w_gate, w_up = (
        pltpu.with_memory_space_constraint(w[0], pltpu.HBM) for w in (gate_weight, up_weight)
    )
    w_down = down_weight[0]
    part = width // 2
    parts = 2 if w_gate.shape[1] % (2 * LANES) == 0 else 1

    me = lax.axis_index(("expert", "tensor")).astype(jnp.uint32)
    rows_of = jnp.asarray(tables(experts, n))
    length = rows_of.shape[1]
    table = lax.dynamic_slice(rows_of, (me, jnp.uint32(0)), (1, length)).reshape(length)

    ring = ring_of(n)
    ahead = [(ring[p], ring[(p + 1) % n]) for p in range(n)]
    behind = [(b, a) for a, b in ahead]

    core = (lax.axis_index("expert") & 1).reshape(1)
    own = prepare(core, tokens, expert_ids.T, gate_units.T)
    wanted = [(other, w) for other in (False, True) for w in (w_gate, w_up)]
    fetched = []

    def fetch_next(after):
        other, w = wanted[len(fetched)]

        def place(tab):
            return (1 - tab[0] if other else tab[0]) * part, slice(None)

        fetched.append(fetch(table, w, (part, w.shape[1]), place, after))

    brought = [own]
    forward = backward = own
    cut = part // 2
    for hop in range(1, n // 2 + 1):
        if hop > 1 and len(fetched) < len(wanted) + 1:
            forward, backward, fetched[-1] = lax.optimization_barrier(
                (forward, backward, fetched[-1])
            )
        if len(fetched) < len(wanted):
            fetch_next(forward)
        if hop < n // 2:
            forward = lax.ppermute(forward, "tensor", ahead)
            backward = lax.ppermute(backward, "tensor", behind)
            brought += [forward, backward]
        else:
            first = lax.ppermute(forward[:, :cut], "tensor", ahead)
            second = lax.ppermute(backward[:, cut:], "tensor", behind)
    while len(fetched) < len(wanted):
        fetch_next(forward)

    first, second, fetched[-1] = lax.optimization_barrier((first, second, fetched[-1]))
    far = jnp.concatenate([first, second], axis=1)
    collected, other = [], []
    for cols in (slice(0, cut), slice(cut, part), slice(part, part + LANES)):
        whole = jnp.zeros((n * rows, cols.stop - cols.start), tokens.dtype)
        for slot, block in enumerate(brought + [far]):
            whole = lax.dynamic_update_slice(whole, block[:, cols], (slot * rows, 0))
        collected.append(whole)
    gate_own, up_own, gate_other, up_other = fetched
    routing = collected[2]
    for q in range(2):
        other.append(lax.ppermute(collected[q], "expert", [(i, i ^ 1) for i in range(experts)]))
    sums = []
    for q in range(2):
        sums = depth_part(collected[q], gate_own, up_own, q, sums)
    sums = depth_part(other[0], gate_other, up_other, 0, sums)

    hidden = [
        hidden_part(table, other[1], gate_other, up_other, 1, sums, n, j, parts)
        for j in range(parts)
    ]
    total = None
    held = [([block], [3]) for block in hidden]
    half = n * rows // 2
    for hop in range(1, n // 2 + 1):
        came = []
        for j in range(parts):
            blocks, slots = held[j]
            if total is not None and hop > 1:
                blocks, total = lax.optimization_barrier((blocks, total))
            forward, backward = blocks[0], blocks[-1]
            if hop < n // 2:
                forward = lax.ppermute(forward, "tensor", ahead)
                backward = lax.ppermute(backward, "tensor", behind)
                held[j] = ([forward, backward], [2 + 2 * hop, 3 + 2 * hop])
            else:
                forward = lax.ppermute(forward[:half], "tensor", ahead)
                backward = lax.ppermute(backward[half:], "tensor", behind)
                held[j] = (forward, backward)
            came.append((blocks, [(slot, j) for slot in slots]))
            if hop > 1 and (hop < n // 2 or j < parts - 1):
                total = down_step(table, total, *came.pop(), w_down, parts)
        if hop == 1:
            own = lax.optimization_barrier([blocks for blocks, _ in came])
            for blocks, (_, places) in zip(own, came):
                total = down_step(table, total, blocks, places, w_down, parts)
    for j in range(parts):
        if j == parts - 1:
            total = down_step(table, total, *came.pop(), w_down, parts)
        total = down_last(
            table, total, *held[j], 2 + n, w_down, j, parts, experts, j == parts - 1
        )

    pieces = [total[0]] + [
        lax.ppermute(total[i], "expert", [(s, s ^ i) for s in range(experts)])
        for i in range(1, experts)
    ]
    mixed = combine(table, pieces, routing, n, 3 + n)
    owners = [
        (e * n + t, (t // group) * n + group * e + t % group)
        for e in range(experts)
        for t in range(n)
    ]
    mixed = lax.ppermute(mixed, ("expert", "tensor"), owners)
    arrived = [mixed[0]]
    for k in range(1, group):
        pairs = [(t, t // group * group + (t + k) % group) for t in range(n)]
        arrived.append(lax.ppermute(mixed[k], "tensor", pairs))
    return assemble(table, arrived)


def solution(mesh):
    return jax.shard_map(
        local,
        mesh=mesh,
        in_specs=(
            P("tensor", None),
            P("tensor", None),
            P("tensor", None),
            P("expert", None, "tensor"),
            P("expert", None, "tensor"),
            P("expert", "tensor", None),
        ),
        out_specs=P("tensor", "expert"),
        check_vma=False,
    )
```

```python
import jax
import jax.numpy as jnp
import numpy as np
from jax import lax
from jax.experimental import pallas as pl
from jax.experimental.pallas import tpu as pltpu
from jax.sharding import PartitionSpec as P

LANES = 128
WHOLE = pl.BlockSpec(memory_space=pltpu.VMEM)


def ring_of(count):
    return list(range(0, count, 2)) + list(range(count - 1, 0, -2))


def hop_list(count):
    hops = [0]
    for hop in range(1, count // 2):
        hops += [hop, -hop]
    return hops + [count // 2]


def tables(experts, n):
    ring = ring_of(n)
    hops = hop_list(n)
    group = n // experts
    rows = []
    for e in range(experts):
        for t in range(n):
            place = ring.index(t)
            sources = [ring[(place - hop) % n] for hop in hops]
            mine = [sources.index(group * e + (i + t) % group) for i in range(group)]
            rows.append([e % 2, e, t % group] + sources + mine)
    return np.array(rows, np.int32)


def params(megabytes):
    return pltpu.CompilerParams(vmem_limit_bytes=megabytes << 20)


def dot(a, b):
    return jnp.dot(a, b, preferred_element_type=jnp.float32)


def dot_nt(a, b):
    return lax.dot_general(a, b, (((1,), (1,)), ((), ())), preferred_element_type=jnp.float32)


def prepare(core, tokens, expert_ids, gate_units):
    rows, width = tokens.shape
    part = width // 2

    def kernel(core_ref, tokens_ref, ids_ref, units_ref, out, ids, units, sems):
        start = pl.multiple_of(core_ref[0] * part, part)
        copies = [
            pltpu.make_async_copy(source, target, sems.at[i])
            for i, (source, target) in enumerate(
                [
                    (ids_ref, ids),
                    (units_ref, units),
                    (tokens_ref.at[:, pl.ds(start, part)], out.at[:, :part]),
                ]
            )
        ]
        for copy in copies:
            copy.start()
        copies[0].wait()
        copies[1].wait()
        number = units[...]
        lines = [ids[...], number >> 8, number & 255]
        route = jnp.concatenate(
            [line.astype(jnp.float32) for line in lines] + [jnp.zeros((2, rows), jnp.float32)], axis=0
        )
        route = jnp.concatenate([route, jnp.zeros((8, LANES - rows), jnp.float32)], axis=1)
        route = jnp.concatenate([route, jnp.zeros((LANES - 8, LANES), jnp.float32)], axis=0)
        out[:, part:] = route.T[:rows, :].astype(jnp.bfloat16)
        copies[2].wait()

    hbm = pl.BlockSpec(memory_space=pltpu.HBM)
    return pl.pallas_call(
        kernel,
        grid_spec=pltpu.PrefetchScalarGridSpec(
            num_scalar_prefetch=1,
            in_specs=[hbm] * 3,
            out_specs=WHOLE,
            scratch_shapes=[
                pltpu.VMEM((2, rows), jnp.int32),
                pltpu.VMEM((2, rows), jnp.int32),
                pltpu.SemaphoreType.DMA((3,)),
            ],
        ),
        out_shape=pltpu.VMEM((rows, part + LANES), tokens.dtype),
        compiler_params=params(4),
        name="prepare",
    )(core, *[pltpu.with_memory_space_constraint(a, pltpu.HBM) for a in (tokens, expert_ids, gate_units)])


def bring(w_ref, out, sems, rows, columns):
    pieces = sems.shape[0]
    step = out.shape[0] // pieces
    copies = []
    for i in range(pieces):
        start = rows + i * step
        if not isinstance(start, int):
            start = pl.multiple_of(start, step)
        copies.append(
            pltpu.make_async_copy(
                w_ref.at[pl.ds(start, step), columns], out.at[pl.ds(i * step, step), :], sems.at[i]
            )
        )
    for copy in copies:
        copy.start()
    for copy in copies:
        copy.wait()


def fetch(table, weight, shape, place, after):
    pieces = next(k for k in (8, 4, 2, 1) if shape[0] % (k * 16) == 0)

    def kernel(tab, w_ref, after_ref, out, sems):
        del after_ref
        bring(w_ref, out, sems, *place(tab))

    return pl.pallas_call(
        kernel,
        grid_spec=pltpu.PrefetchScalarGridSpec(
            num_scalar_prefetch=1,
            in_specs=[
                pl.BlockSpec(memory_space=pltpu.HBM),
                pl.BlockSpec(memory_space=pl.ANY),
            ],
            out_specs=WHOLE,
            scratch_shapes=[pltpu.SemaphoreType.DMA((pieces,))],
        ),
        out_shape=pltpu.VMEM(shape, weight.dtype),
        compiler_params=params(4),
        cost_estimate=pl.CostEstimate(
            flops=0, bytes_accessed=4 * shape[0] * shape[1], transcendentals=0
        ),
        name="fetch",
    )(table, weight, after)


def column_tiles(units):
    size = 256 if units % 256 == 0 else units
    return [slice(i, i + size) for i in range(0, units, size)]


def depth_part(x, w_gate, w_up, q, sums):
    m, depth = x.shape
    units = w_gate.shape[1]
    rows = slice(q * depth, (q + 1) * depth)

    def kernel(x_ref, g_ref, u_ref, *refs):
        gate, up = refs[-2:]
        for cols in column_tiles(units):
            for w_ref, out, before in ((g_ref, gate, 0), (u_ref, up, 1)):
                product = dot(x_ref[...], w_ref[rows, cols])
                if sums:
                    product += refs[before][:, cols]
                out[:, cols] = product

    out = jax.ShapeDtypeStruct((m, units), jnp.float32)
    return pl.pallas_call(
        kernel,
        in_specs=[WHOLE] * (3 + len(sums)),
        out_specs=[WHOLE, WHOLE],
        out_shape=[out, out],
        compiler_params=params(8),
        cost_estimate=pl.CostEstimate(
            flops=4 * m * depth * units, bytes_accessed=4 * depth * units, transcendentals=0
        ),
        name="gate_up",
    )(x, w_gate, w_up, *sums)


def hidden_part(table, x, w_gate, w_up, q, sums, n, j, parts):
    m, depth = x.shape
    units = w_gate.shape[1] // parts
    rows = m // n
    deep = slice(q * depth, (q + 1) * depth)

    def kernel(tab, x_ref, g_ref, u_ref, gate_ref, up_ref, out):
        for cols in column_tiles(units):
            there = slice(j * units + cols.start, j * units + cols.stop)
            gate = gate_ref[:, there] + dot(x_ref[...], g_ref[deep, there])
            up = up_ref[:, there] + dot(x_ref[...], u_ref[deep, there])
            hidden = (gate * jax.nn.sigmoid(gate) * up).astype(out.dtype)
            for r in range(n):
                out[tab[3 + r], :, cols] = hidden[r * rows : (r + 1) * rows, :]

    return pl.pallas_call(
        kernel,
        grid_spec=pltpu.PrefetchScalarGridSpec(
            num_scalar_prefetch=1, in_specs=[WHOLE] * 5, out_specs=WHOLE
        ),
        out_shape=jax.ShapeDtypeStruct((n, rows, units), jnp.bfloat16),
        compiler_params=params(12),
        cost_estimate=pl.CostEstimate(
            flops=4 * m * depth * units, bytes_accessed=4 * depth * units, transcendentals=m * units
        ),
        name="hidden",
    )(table, x, w_gate, w_up, *sums).reshape(m, units)


def down_step(table, total, blocks, places, w_down, parts):
    m, depth = blocks[0].shape
    feats = w_down.shape[0]
    count = len(blocks)

    def kernel(tab, *refs):
        lhs, w_ref, out = refs[:count], refs[count], refs[-1]
        for i, (slot, j) in enumerate(places):
            start = pl.multiple_of((tab[slot] * parts + j) * depth, depth)
            product = dot_nt(lhs[i][...], w_ref[:, pl.ds(start, depth)])
            if i:
                out[...] += product
            elif total is None:
                out[...] = product
            else:
                out[...] = refs[count + 1][...] + product

    more = [] if total is None else [total]
    return pl.pallas_call(
        kernel,
        grid_spec=pltpu.PrefetchScalarGridSpec(
            num_scalar_prefetch=1,
            in_specs=[WHOLE] * (count + 1 + len(more)),
            out_specs=WHOLE,
        ),
        out_shape=jax.ShapeDtypeStruct((m, feats), jnp.float32),
        compiler_params=params(8),
        cost_estimate=pl.CostEstimate(
            flops=count * m * depth, bytes_accessed=0, transcendentals=0
        ),
        name="down",
    )(table, *blocks, w_down, *more)


def down_last(table, total, first, second, slot, w_down, j, parts, experts, final):
    half, depth = first.shape
    m = 2 * half
    feats = w_down.shape[0]
    share = m // experts

    def kernel(tab, a_ref, b_ref, w_ref, total_ref, *refs):
        target = refs[-1] if final else refs[0]
        there = pl.ds(pl.multiple_of((tab[slot] * parts + j) * depth, depth), depth)
        target[:half, :] = total_ref[:half, :] + dot_nt(a_ref[...], w_ref[:, there])
        target[half:, :] = total_ref[half:, :] + dot_nt(b_ref[...], w_ref[:, there])
        if final:
            for i in range(experts):
                start = pl.multiple_of((tab[1] ^ i) * share, share)
                refs[i][...] = target[pl.ds(start, share), :].astype(jnp.bfloat16)

    if final:
        out_shape = [jax.ShapeDtypeStruct((share, feats), jnp.bfloat16)] * experts
        out_specs = [WHOLE] * experts
    else:
        out_shape = jax.ShapeDtypeStruct((m, feats), jnp.float32)
        out_specs = WHOLE
    return pl.pallas_call(
        kernel,
        grid_spec=pltpu.PrefetchScalarGridSpec(
            num_scalar_prefetch=1,
            in_specs=[WHOLE] * 4,
            out_specs=out_specs,
            scratch_shapes=[pltpu.VMEM((m, feats), jnp.float32)] if final else [],
        ),
        out_shape=out_shape,
        compiler_params=params(8),
        cost_estimate=pl.CostEstimate(
            flops=m * depth, bytes_accessed=0, transcendentals=0
        ),
        name="down_last",
    )(table, first, second, w_down, total)


def combine(table, pieces, routing, n, base):
    experts = len(pieces)
    share, feats = pieces[0].shape
    rows = routing.shape[0] // n
    group = share // rows

    def kernel(tab, *refs):
        ins, route_ref, outs, route = refs[:experts], refs[experts], refs[experts + 1 : -1], refs[-1]
        route[...] = route_ref[...].astype(jnp.float32)
        for k in range(group):
            block = lax.rem(k + tab[2], group)
            info = route[pl.ds(pl.multiple_of(tab[base + k] * rows, rows), rows), :]
            unit0 = info[:, 2:3] * 256.0 + info[:, 4:5]
            unit1 = info[:, 3:4] * 256.0 + info[:, 5:6]
            whole = unit0 + unit1
            share0, share1 = unit0 / whole, unit1 / whole
            mixed = jnp.zeros((rows, feats), jnp.float32)
            for i in range(experts):
                name = (tab[1] ^ i).astype(jnp.float32)
                weight = jnp.where(info[:, 0:1] == name, share0, 0.0)
                weight += jnp.where(info[:, 1:2] == name, share1, 0.0)
                mixed += weight * ins[i][block].astype(jnp.float32)
            outs[k][...] = mixed.astype(jnp.bfloat16)

    return pl.pallas_call(
        kernel,
        grid_spec=pltpu.PrefetchScalarGridSpec(
            num_scalar_prefetch=1,
            in_specs=[WHOLE] * (experts + 1),
            out_specs=[WHOLE] * group,
            scratch_shapes=[pltpu.VMEM(routing.shape, jnp.float32)],
        ),
        out_shape=[jax.ShapeDtypeStruct((rows, feats), jnp.bfloat16)] * group,
        compiler_params=params(16),
        name="combine",
    )(table, *[piece.reshape(group, rows, feats) for piece in pieces], routing)


def local(tokens, expert_ids, gate_units, gate_weight, up_weight, down_weight):
    experts = lax.axis_size("expert")
    n = lax.axis_size("tensor")
    group = n // experts
    rows, width = tokens.shape
    w_gate, w_up = (
        pltpu.with_memory_space_constraint(w[0], pltpu.HBM) for w in (gate_weight, up_weight)
    )
    w_down = down_weight[0]
    part = width // 2
    parts = 2 if w_gate.shape[1] % (2 * LANES) == 0 else 1

    me = lax.axis_index(("expert", "tensor")).astype(jnp.uint32)
    rows_of = jnp.asarray(tables(experts, n))
    length = rows_of.shape[1]
    table = lax.dynamic_slice(rows_of, (me, jnp.uint32(0)), (1, length)).reshape(length)

    ring = ring_of(n)
    ahead = [(ring[p], ring[(p + 1) % n]) for p in range(n)]
    behind = [(b, a) for a, b in ahead]

    core = (lax.axis_index("expert") & 1).reshape(1)
    own = prepare(core, tokens, expert_ids.T, gate_units.T)
    wanted = [(other, w) for other in (False, True) for w in (w_gate, w_up)]
    fetched = []

    def fetch_next(after):
        other, w = wanted[len(fetched)]

        def place(tab):
            return (1 - tab[0] if other else tab[0]) * part, slice(None)

        fetched.append(fetch(table, w, (part, w.shape[1]), place, after))

    brought = [own]
    forward = backward = own
    cut = part // 2
    for hop in range(1, n // 2 + 1):
        if hop > 1 and len(fetched) < len(wanted) + 1:
            forward, backward, fetched[-1] = lax.optimization_barrier(
                (forward, backward, fetched[-1])
            )
        if len(fetched) < len(wanted):
            fetch_next(forward)
        if hop < n // 2:
            forward = lax.ppermute(forward, "tensor", ahead)
            backward = lax.ppermute(backward, "tensor", behind)
            brought += [forward, backward]
        else:
            first = lax.ppermute(forward[:, :cut], "tensor", ahead)
            second = lax.ppermute(backward[:, cut:], "tensor", behind)
    while len(fetched) < len(wanted):
        fetch_next(forward)

    first, second, fetched[-1] = lax.optimization_barrier((first, second, fetched[-1]))
    far = jnp.concatenate([first, second], axis=1)
    collected, other = [], []
    for cols in (slice(0, cut), slice(cut, part), slice(part, part + LANES)):
        whole = jnp.zeros((n * rows, cols.stop - cols.start), tokens.dtype)
        for slot, block in enumerate(brought + [far]):
            whole = lax.dynamic_update_slice(whole, block[:, cols], (slot * rows, 0))
        collected.append(whole)
    gate_own, up_own, gate_other, up_other = fetched
    routing = collected[2]
    for q in range(2):
        other.append(lax.ppermute(collected[q], "expert", [(i, i ^ 1) for i in range(experts)]))
    sums = []
    for q in range(2):
        sums = depth_part(collected[q], gate_own, up_own, q, sums)
    sums = depth_part(other[0], gate_other, up_other, 0, sums)

    hidden = [
        hidden_part(table, other[1], gate_other, up_other, 1, sums, n, j, parts)
        for j in range(parts)
    ]
    total = None
    held = [([block], [3]) for block in hidden]
    half = n * rows // 2
    for hop in range(1, n // 2 + 1):
        came = []
        for j in range(parts):
            blocks, slots = held[j]
            if total is not None and hop > 1:
                blocks, total = lax.optimization_barrier((blocks, total))
            forward, backward = blocks[0], blocks[-1]
            if hop < n // 2:
                forward = lax.ppermute(forward, "tensor", ahead)
                backward = lax.ppermute(backward, "tensor", behind)
                held[j] = ([forward, backward], [2 + 2 * hop, 3 + 2 * hop])
            else:
                forward = lax.ppermute(forward[:half], "tensor", ahead)
                backward = lax.ppermute(backward[half:], "tensor", behind)
                held[j] = (forward, backward)
            came.append((blocks, [(slot, j) for slot in slots]))
            if hop > 1 and (hop < n // 2 or j < parts - 1):
                total = down_step(table, total, *came.pop(), w_down, parts)
        if hop == 1:
            own = lax.optimization_barrier([blocks for blocks, _ in came])
            for blocks, (_, places) in zip(own, came):
                total = down_step(table, total, blocks, places, w_down, parts)
    for j in range(parts):
        if j == parts - 1:
            total = down_step(table, total, *came.pop(), w_down, parts)
        total = down_last(
            table, total, *held[j], 2 + n, w_down, j, parts, experts, j == parts - 1
        )

    pieces = [total[0]] + [
        lax.ppermute(total[i], "expert", [(s, s ^ i) for s in range(experts)])
        for i in range(1, experts)
    ]
    mixed = combine(table, pieces, routing, n, 3 + n)
    arrived = []
    for k in range(group):
        pairs = []
        for e in range(experts):
            for t in range(n):
                pairs.append((e * n + t, (t // group) * n + group * e + (k + t) % group))
        arrived.append(lax.ppermute(mixed[k], ("expert", "tensor"), pairs))
    own = lax.axis_index("tensor") & (group - 1)
    spots = [(own - s) & (group - 1) for s in range(group)]
    return jnp.concatenate([lax.select_n(spot, *arrived) for spot in spots], axis=1)


def solution(mesh):
    return jax.shard_map(
        local,
        mesh=mesh,
        in_specs=(
            P("tensor", None),
            P("tensor", None),
            P("tensor", None),
            P("expert", None, "tensor"),
            P("expert", None, "tensor"),
            P("expert", "tensor", None),
        ),
        out_specs=P("tensor", "expert"),
        check_vma=False,
    )
```

```python
import jax
import jax.numpy as jnp
import numpy as np
from jax import lax
from jax.experimental import pallas as pl
from jax.experimental.pallas import tpu as pltpu
from jax.sharding import PartitionSpec as P

LANES = 128
WHOLE = pl.BlockSpec(memory_space=pltpu.VMEM)


def ring_of(count):
    return list(range(0, count, 2)) + list(range(count - 1, 0, -2))


def hop_list(count):
    hops = [0]
    for hop in range(1, count // 2):
        hops += [hop, -hop]
    return hops + [count // 2]


def tables(experts, n):
    ring = ring_of(n)
    hops = hop_list(n)
    group = n // experts
    rows = []
    for e in range(experts):
        for t in range(n):
            place = ring.index(t)
            sources = [ring[(place - hop) % n] for hop in hops]
            mine = [sources.index(group * e + (i + t) % group) for i in range(group)]
            rows.append([e % 2, e, t % group] + sources + mine)
    return np.array(rows, np.int32)


def params(megabytes):
    return pltpu.CompilerParams(vmem_limit_bytes=megabytes << 20)


def dot(a, b):
    return jnp.dot(a, b, preferred_element_type=jnp.float32)


def dot_nt(a, b):
    return lax.dot_general(a, b, (((1,), (1,)), ((), ())), preferred_element_type=jnp.float32)


def prepare(core, tokens, expert_ids, gate_units):
    rows, width = tokens.shape
    part = width // 2

    def kernel(core_ref, tokens_ref, ids_ref, units_ref, out, ids, units, sems):
        start = pl.multiple_of(core_ref[0] * part, part)
        copies = [
            pltpu.make_async_copy(source, target, sems.at[i])
            for i, (source, target) in enumerate(
                [
                    (ids_ref, ids),
                    (units_ref, units),
                    (tokens_ref.at[:, pl.ds(start, part)], out.at[:, :part]),
                ]
            )
        ]
        for copy in copies:
            copy.start()
        copies[0].wait()
        copies[1].wait()
        number = units[...]
        lines = [ids[...], number >> 8, number & 255]
        route = jnp.concatenate(
            [line.astype(jnp.float32) for line in lines] + [jnp.zeros((2, rows), jnp.float32)], axis=0
        )
        route = jnp.concatenate([route, jnp.zeros((8, LANES - rows), jnp.float32)], axis=1)
        route = jnp.concatenate([route, jnp.zeros((LANES - 8, LANES), jnp.float32)], axis=0)
        out[:, part:] = route.T[:rows, :].astype(jnp.bfloat16)
        copies[2].wait()

    hbm = pl.BlockSpec(memory_space=pltpu.HBM)
    return pl.pallas_call(
        kernel,
        grid_spec=pltpu.PrefetchScalarGridSpec(
            num_scalar_prefetch=1,
            in_specs=[hbm] * 3,
            out_specs=WHOLE,
            scratch_shapes=[
                pltpu.VMEM((2, rows), jnp.int32),
                pltpu.VMEM((2, rows), jnp.int32),
                pltpu.SemaphoreType.DMA((3,)),
            ],
        ),
        out_shape=pltpu.VMEM((rows, part + LANES), tokens.dtype),
        compiler_params=params(4),
        name="prepare",
    )(core, *[pltpu.with_memory_space_constraint(a, pltpu.HBM) for a in (tokens, expert_ids, gate_units)])


def bring(w_ref, out, sems, rows, columns):
    pieces = sems.shape[0]
    step = out.shape[0] // pieces
    copies = []
    for i in range(pieces):
        start = rows + i * step
        if not isinstance(start, int):
            start = pl.multiple_of(start, step)
        copies.append(
            pltpu.make_async_copy(
                w_ref.at[pl.ds(start, step), columns], out.at[pl.ds(i * step, step), :], sems.at[i]
            )
        )
    for copy in copies:
        copy.start()
    for copy in copies:
        copy.wait()


def fetch(table, weight, shape, place, after):
    pieces = next(k for k in (8, 4, 2, 1) if shape[0] % (k * 16) == 0)

    def kernel(tab, w_ref, after_ref, out, sems):
        del after_ref
        bring(w_ref, out, sems, *place(tab))

    return pl.pallas_call(
        kernel,
        grid_spec=pltpu.PrefetchScalarGridSpec(
            num_scalar_prefetch=1,
            in_specs=[
                pl.BlockSpec(memory_space=pltpu.HBM),
                pl.BlockSpec(memory_space=pl.ANY),
            ],
            out_specs=WHOLE,
            scratch_shapes=[pltpu.SemaphoreType.DMA((pieces,))],
        ),
        out_shape=pltpu.VMEM(shape, weight.dtype),
        compiler_params=params(4),
        cost_estimate=pl.CostEstimate(
            flops=0, bytes_accessed=4 * shape[0] * shape[1], transcendentals=0
        ),
        name="fetch",
    )(table, weight, after)


def column_tiles(units):
    size = 256 if units % 256 == 0 else units
    return [slice(i, i + size) for i in range(0, units, size)]


def hidden_part(table, own, other, weights, n, j, parts):
    m, depth = other.shape
    units = weights[0].shape[1] // parts
    rows = m // n

    def kernel(tab, own_ref, other_ref, gate_own, up_own, gate_other, up_other, out):
        for cols in column_tiles(units):
            there = slice(j * units + cols.start, j * units + cols.stop)
            gate = dot(own_ref[:, :depth], gate_own[:, there])
            gate += dot(other_ref[...], gate_other[:, there])
            up = dot(own_ref[:, :depth], up_own[:, there])
            up += dot(other_ref[...], up_other[:, there])
            hidden = (gate * jax.nn.sigmoid(gate) * up).astype(out.dtype)
            for r in range(n):
                out[tab[3 + r], :, cols] = hidden[r * rows : (r + 1) * rows, :]

    return pl.pallas_call(
        kernel,
        grid_spec=pltpu.PrefetchScalarGridSpec(
            num_scalar_prefetch=1, in_specs=[WHOLE] * 6, out_specs=WHOLE
        ),
        out_shape=jax.ShapeDtypeStruct((n, rows, units), jnp.bfloat16),
        compiler_params=params(12),
        cost_estimate=pl.CostEstimate(
            flops=8 * m * depth * units, bytes_accessed=8 * depth * units, transcendentals=m * units
        ),
        name="hidden",
    )(table, own, other, *weights).reshape(m, units)


def down_step(table, total, blocks, places, w_down, parts):
    m, depth = blocks[0].shape
    feats = w_down.shape[0]
    count = len(blocks)

    def kernel(tab, *refs):
        lhs, w_ref, out = refs[:count], refs[count], refs[-1]
        for i, (slot, j) in enumerate(places):
            start = pl.multiple_of((tab[slot] * parts + j) * depth, depth)
            product = dot_nt(lhs[i][...], w_ref[:, pl.ds(start, depth)])
            if i:
                out[...] += product
            elif total is None:
                out[...] = product
            else:
                out[...] = refs[count + 1][...] + product

    more = [] if total is None else [total]
    return pl.pallas_call(
        kernel,
        grid_spec=pltpu.PrefetchScalarGridSpec(
            num_scalar_prefetch=1,
            in_specs=[WHOLE] * (count + 1 + len(more)),
            out_specs=WHOLE,
        ),
        out_shape=jax.ShapeDtypeStruct((m, feats), jnp.float32),
        compiler_params=params(8),
        cost_estimate=pl.CostEstimate(
            flops=count * m * depth, bytes_accessed=0, transcendentals=0
        ),
        name="down",
    )(table, *blocks, w_down, *more)


def down_last(table, total, first, second, slot, w_down, j, parts, experts, final):
    half, depth = first.shape
    m = 2 * half
    feats = w_down.shape[0]
    share = m // experts

    def kernel(tab, a_ref, b_ref, w_ref, total_ref, *refs):
        target = refs[-1] if final else refs[0]
        there = pl.ds(pl.multiple_of((tab[slot] * parts + j) * depth, depth), depth)
        target[:half, :] = total_ref[:half, :] + dot_nt(a_ref[...], w_ref[:, there])
        target[half:, :] = total_ref[half:, :] + dot_nt(b_ref[...], w_ref[:, there])
        if final:
            for i in range(experts):
                start = pl.multiple_of((tab[1] ^ i) * share, share)
                refs[i][...] = target[pl.ds(start, share), :].astype(jnp.bfloat16)

    if final:
        out_shape = [jax.ShapeDtypeStruct((share, feats), jnp.bfloat16)] * experts
        out_specs = [WHOLE] * experts
    else:
        out_shape = jax.ShapeDtypeStruct((m, feats), jnp.float32)
        out_specs = WHOLE
    return pl.pallas_call(
        kernel,
        grid_spec=pltpu.PrefetchScalarGridSpec(
            num_scalar_prefetch=1,
            in_specs=[WHOLE] * 4,
            out_specs=out_specs,
            scratch_shapes=[pltpu.VMEM((m, feats), jnp.float32)] if final else [],
        ),
        out_shape=out_shape,
        compiler_params=params(8),
        cost_estimate=pl.CostEstimate(
            flops=m * depth, bytes_accessed=0, transcendentals=0
        ),
        name="down_last",
    )(table, first, second, w_down, total)


def combine(table, pieces, routing, n, base):
    experts = len(pieces)
    share, feats = pieces[0].shape
    rows = routing.shape[0] // n
    group = share // rows

    def kernel(tab, *refs):
        ins, route_ref, outs, route = refs[:experts], refs[experts], refs[experts + 1 : -1], refs[-1]
        route[...] = route_ref[...].astype(jnp.float32)
        for k in range(group):
            block = lax.rem(k + tab[2], group)
            info = route[pl.ds(pl.multiple_of(tab[base + k] * rows, rows), rows), :]
            unit0 = info[:, 2:3] * 256.0 + info[:, 4:5]
            unit1 = info[:, 3:4] * 256.0 + info[:, 5:6]
            whole = unit0 + unit1
            share0, share1 = unit0 / whole, unit1 / whole
            mixed = jnp.zeros((rows, feats), jnp.float32)
            for i in range(experts):
                name = (tab[1] ^ i).astype(jnp.float32)
                weight = jnp.where(info[:, 0:1] == name, share0, 0.0)
                weight += jnp.where(info[:, 1:2] == name, share1, 0.0)
                mixed += weight * ins[i][block].astype(jnp.float32)
            outs[k][...] = mixed.astype(jnp.bfloat16)

    return pl.pallas_call(
        kernel,
        grid_spec=pltpu.PrefetchScalarGridSpec(
            num_scalar_prefetch=1,
            in_specs=[WHOLE] * (experts + 1),
            out_specs=[WHOLE] * group,
            scratch_shapes=[pltpu.VMEM(routing.shape, jnp.float32)],
        ),
        out_shape=[jax.ShapeDtypeStruct((rows, feats), jnp.bfloat16)] * group,
        compiler_params=params(16),
        name="combine",
    )(table, *[piece.reshape(group, rows, feats) for piece in pieces], routing)


def local(tokens, expert_ids, gate_units, gate_weight, up_weight, down_weight):
    experts = lax.axis_size("expert")
    n = lax.axis_size("tensor")
    group = n // experts
    rows, width = tokens.shape
    w_gate, w_up = (
        pltpu.with_memory_space_constraint(w[0], pltpu.HBM) for w in (gate_weight, up_weight)
    )
    w_down = down_weight[0]
    part = width // 2
    parts = 2 if w_gate.shape[1] % (2 * LANES) == 0 else 1

    me = lax.axis_index(("expert", "tensor")).astype(jnp.uint32)
    rows_of = jnp.asarray(tables(experts, n))
    length = rows_of.shape[1]
    table = lax.dynamic_slice(rows_of, (me, jnp.uint32(0)), (1, length)).reshape(length)

    ring = ring_of(n)
    ahead = [(ring[p], ring[(p + 1) % n]) for p in range(n)]
    behind = [(b, a) for a, b in ahead]

    core = (lax.axis_index("expert") & 1).reshape(1)
    own = prepare(core, tokens, expert_ids.T, gate_units.T)
    wanted = [(other, w) for other in (False, True) for w in (w_gate, w_up)]
    fetched = []

    def fetch_next(after):
        other, w = wanted[len(fetched)]

        def place(tab):
            return (1 - tab[0] if other else tab[0]) * part, slice(None)

        fetched.append(fetch(table, w, (part, w.shape[1]), place, after))

    brought = [own]
    forward = backward = own
    cut = part // 2
    for hop in range(1, n // 2 + 1):
        if hop > 1 and len(fetched) < len(wanted) + 1:
            forward, backward, fetched[-1] = lax.optimization_barrier(
                (forward, backward, fetched[-1])
            )
        if len(fetched) < len(wanted):
            fetch_next(forward)
        if hop < n // 2:
            forward = lax.ppermute(forward, "tensor", ahead)
            backward = lax.ppermute(backward, "tensor", behind)
            brought += [forward, backward]
        else:
            first = lax.ppermute(forward[:, :cut], "tensor", ahead)
            second = lax.ppermute(backward[:, cut:], "tensor", behind)
    while len(fetched) < len(wanted):
        fetch_next(forward)

    swap = [(i, i ^ 1) for i in range(experts)]
    brought[-2:], fetched[-2] = lax.optimization_barrier((brought[-2:], fetched[-2]))
    own = jnp.zeros((n * rows, part + LANES), tokens.dtype)
    for slot, block in enumerate(brought):
        own = lax.dynamic_update_slice(own, block, (slot * rows, 0))
    other = lax.ppermute(own[:, :part], "expert", swap)
    first, second, fetched[-1] = lax.optimization_barrier((first, second, fetched[-1]))
    far = jnp.concatenate([first, second], axis=1)
    own = lax.dynamic_update_slice(own, far, ((n - 1) * rows, 0))
    far = lax.ppermute(far[:, :part], "expert", swap)
    other = lax.dynamic_update_slice(other, far, ((n - 1) * rows, 0))
    routing = own[:, part:]
    gate_own, up_own, gate_other, up_other = fetched
    weights = (gate_own, up_own, gate_other, up_other)

    hidden = [hidden_part(table, own, other, weights, n, j, parts) for j in range(parts)]
    total = None
    held = [([block], [3]) for block in hidden]
    half = n * rows // 2
    for hop in range(1, n // 2 + 1):
        came = []
        for j in range(parts):
            blocks, slots = held[j]
            if total is not None and hop > 1:
                blocks, total = lax.optimization_barrier((blocks, total))
            forward, backward = blocks[0], blocks[-1]
            if hop < n // 2:
                forward = lax.ppermute(forward, "tensor", ahead)
                backward = lax.ppermute(backward, "tensor", behind)
                held[j] = ([forward, backward], [2 + 2 * hop, 3 + 2 * hop])
            else:
                forward = lax.ppermute(forward[:half], "tensor", ahead)
                backward = lax.ppermute(backward[half:], "tensor", behind)
                held[j] = (forward, backward)
            came.append((blocks, [(slot, j) for slot in slots]))
            if hop > 1 and (hop < n // 2 or j < parts - 1):
                total = down_step(table, total, *came.pop(), w_down, parts)
        if hop == 1:
            own = lax.optimization_barrier([blocks for blocks, _ in came])
            for blocks, (_, places) in zip(own, came):
                total = down_step(table, total, blocks, places, w_down, parts)
    for j in range(parts):
        if j == parts - 1:
            total = down_step(table, total, *came.pop(), w_down, parts)
        total = down_last(
            table, total, *held[j], 2 + n, w_down, j, parts, experts, j == parts - 1
        )

    pieces = [total[0]] + [
        lax.ppermute(total[i], "expert", [(s, s ^ i) for s in range(experts)])
        for i in range(1, experts)
    ]
    mixed = combine(table, pieces, routing, n, 3 + n)
    arrived = []
    for k in range(group):
        pairs = []
        for e in range(experts):
            for t in range(n):
                pairs.append((e * n + t, (t // group) * n + group * e + (k + t) % group))
        arrived.append(lax.ppermute(mixed[k], ("expert", "tensor"), pairs))
    own = lax.axis_index("tensor") & (group - 1)
    spots = [(own - s) & (group - 1) for s in range(group)]
    return jnp.concatenate([lax.select_n(spot, *arrived) for spot in spots], axis=1)


def solution(mesh):
    return jax.shard_map(
        local,
        mesh=mesh,
        in_specs=(
            P("tensor", None),
            P("tensor", None),
            P("tensor", None),
            P("expert", None, "tensor"),
            P("expert", None, "tensor"),
            P("expert", "tensor", None),
        ),
        out_specs=P("tensor", "expert"),
        check_vma=False,
    )
```

```python
import jax
import jax.numpy as jnp
import numpy as np
from jax import lax
from jax.experimental import pallas as pl
from jax.experimental.pallas import tpu as pltpu
from jax.sharding import PartitionSpec as P

LANES = 128
WHOLE = pl.BlockSpec(memory_space=pltpu.VMEM)


def ring_of(count):
    return list(range(0, count, 2)) + list(range(count - 1, 0, -2))


def hop_list(count):
    hops = [0]
    for hop in range(1, count // 2):
        hops += [hop, -hop]
    return hops + [count // 2]


def tables(experts, n):
    ring = ring_of(n)
    hops = hop_list(n)
    group = n // experts
    rows = []
    for e in range(experts):
        for t in range(n):
            place = ring.index(t)
            sources = [ring[(place - hop) % n] for hop in hops]
            mine = [sources.index(group * e + (i + t) % group) for i in range(group)]
            rows.append([e % 2, e, t % group] + sources + mine)
    return np.array(rows, np.int32)


def params(megabytes):
    return pltpu.CompilerParams(vmem_limit_bytes=megabytes << 20)


def dot(a, b):
    return jnp.dot(a, b, preferred_element_type=jnp.float32)


def dot_nt(a, b):
    return lax.dot_general(a, b, (((1,), (1,)), ((), ())), preferred_element_type=jnp.float32)


def prepare(core, tokens, expert_ids, gate_units):
    rows, width = tokens.shape
    part = width // 2

    def kernel(core_ref, tokens_ref, ids_ref, units_ref, out, ids, units, sems):
        start = pl.multiple_of(core_ref[0] * part, part)
        copies = [
            pltpu.make_async_copy(source, target, sems.at[i])
            for i, (source, target) in enumerate(
                [
                    (ids_ref, ids),
                    (units_ref, units),
                    (tokens_ref.at[:, pl.ds(start, part)], out.at[:, :part]),
                ]
            )
        ]
        for copy in copies:
            copy.start()
        copies[0].wait()
        copies[1].wait()
        number = units[...]
        lines = [ids[...], number >> 8, number & 255]
        route = jnp.concatenate(
            [line.astype(jnp.float32) for line in lines] + [jnp.zeros((2, rows), jnp.float32)], axis=0
        )
        route = jnp.concatenate([route, jnp.zeros((8, LANES - rows), jnp.float32)], axis=1)
        route = jnp.concatenate([route, jnp.zeros((LANES - 8, LANES), jnp.float32)], axis=0)
        out[:, part:] = route.T[:rows, :].astype(jnp.bfloat16)
        copies[2].wait()

    hbm = pl.BlockSpec(memory_space=pltpu.HBM)
    return pl.pallas_call(
        kernel,
        grid_spec=pltpu.PrefetchScalarGridSpec(
            num_scalar_prefetch=1,
            in_specs=[hbm] * 3,
            out_specs=WHOLE,
            scratch_shapes=[
                pltpu.VMEM((2, rows), jnp.int32),
                pltpu.VMEM((2, rows), jnp.int32),
                pltpu.SemaphoreType.DMA((3,)),
            ],
        ),
        out_shape=pltpu.VMEM((rows, part + LANES), tokens.dtype),
        compiler_params=params(4),
        name="prepare",
    )(core, *[pltpu.with_memory_space_constraint(a, pltpu.HBM) for a in (tokens, expert_ids, gate_units)])


def bring(w_ref, out, sems, rows, columns):
    pieces = sems.shape[0]
    step = out.shape[0] // pieces
    copies = []
    for i in range(pieces):
        start = rows + i * step
        if not isinstance(start, int):
            start = pl.multiple_of(start, step)
        copies.append(
            pltpu.make_async_copy(
                w_ref.at[pl.ds(start, step), columns], out.at[pl.ds(i * step, step), :], sems.at[i]
            )
        )
    for copy in copies:
        copy.start()
    for copy in copies:
        copy.wait()


def fetch(table, weight, shape, place, after):
    pieces = next(k for k in (8, 4, 2, 1) if shape[0] % (k * 16) == 0)

    def kernel(tab, w_ref, after_ref, out, sems):
        del after_ref
        bring(w_ref, out, sems, *place(tab))

    return pl.pallas_call(
        kernel,
        grid_spec=pltpu.PrefetchScalarGridSpec(
            num_scalar_prefetch=1,
            in_specs=[
                pl.BlockSpec(memory_space=pltpu.HBM),
                pl.BlockSpec(memory_space=pl.ANY),
            ],
            out_specs=WHOLE,
            scratch_shapes=[pltpu.SemaphoreType.DMA((pieces,))],
        ),
        out_shape=pltpu.VMEM(shape, weight.dtype),
        compiler_params=params(4),
        cost_estimate=pl.CostEstimate(
            flops=0, bytes_accessed=4 * shape[0] * shape[1], transcendentals=0
        ),
        name="fetch",
    )(table, weight, after)


def column_tiles(units):
    size = 256 if units % 256 == 0 else units
    return [slice(i, i + size) for i in range(0, units, size)]


def depth_part(x, w_gate, w_up, q, sums):
    m, depth = x.shape
    units = w_gate.shape[1]
    rows = slice(q * depth, (q + 1) * depth)

    def kernel(x_ref, g_ref, u_ref, *refs):
        gate, up = refs[-2:]
        for cols in column_tiles(units):
            for w_ref, out, before in ((g_ref, gate, 0), (u_ref, up, 1)):
                product = dot(x_ref[...], w_ref[rows, cols])
                if sums:
                    product += refs[before][:, cols]
                out[:, cols] = product

    out = jax.ShapeDtypeStruct((m, units), jnp.float32)
    return pl.pallas_call(
        kernel,
        in_specs=[WHOLE] * (3 + len(sums)),
        out_specs=[WHOLE, WHOLE],
        out_shape=[out, out],
        compiler_params=params(8),
        cost_estimate=pl.CostEstimate(
            flops=4 * m * depth * units, bytes_accessed=4 * depth * units, transcendentals=0
        ),
        name="gate_up",
    )(x, w_gate, w_up, *sums)


def hidden_part(table, x, w_gate, w_up, q, sums, n, j, parts):
    m, depth = x.shape
    units = w_gate.shape[1] // parts
    rows = m // n
    deep = slice(q * depth, (q + 1) * depth)

    def kernel(tab, x_ref, g_ref, u_ref, gate_ref, up_ref, out):
        for cols in column_tiles(units):
            there = slice(j * units + cols.start, j * units + cols.stop)
            gate = gate_ref[:, there] + dot(x_ref[...], g_ref[deep, there])
            up = up_ref[:, there] + dot(x_ref[...], u_ref[deep, there])
            hidden = (gate * jax.nn.sigmoid(gate) * up).astype(out.dtype)
            for r in range(n):
                out[tab[3 + r], :, cols] = hidden[r * rows : (r + 1) * rows, :]

    return pl.pallas_call(
        kernel,
        grid_spec=pltpu.PrefetchScalarGridSpec(
            num_scalar_prefetch=1, in_specs=[WHOLE] * 5, out_specs=WHOLE
        ),
        out_shape=jax.ShapeDtypeStruct((n, rows, units), jnp.bfloat16),
        compiler_params=params(12),
        cost_estimate=pl.CostEstimate(
            flops=4 * m * depth * units, bytes_accessed=4 * depth * units, transcendentals=m * units
        ),
        name="hidden",
    )(table, x, w_gate, w_up, *sums).reshape(m, units)


def down_step(table, total, blocks, places, w_down, parts):
    m, depth = blocks[0].shape
    feats = w_down.shape[0]
    count = len(blocks)

    def kernel(tab, *refs):
        lhs, w_ref, out = refs[:count], refs[count], refs[-1]
        for i, (slot, j) in enumerate(places):
            start = pl.multiple_of((tab[slot] * parts + j) * depth, depth)
            product = dot_nt(lhs[i][...], w_ref[:, pl.ds(start, depth)])
            if i:
                out[...] += product
            elif total is None:
                out[...] = product
            else:
                out[...] = refs[count + 1][...] + product

    more = [] if total is None else [total]
    return pl.pallas_call(
        kernel,
        grid_spec=pltpu.PrefetchScalarGridSpec(
            num_scalar_prefetch=1,
            in_specs=[WHOLE] * (count + 1 + len(more)),
            out_specs=WHOLE,
        ),
        out_shape=jax.ShapeDtypeStruct((m, feats), jnp.float32),
        compiler_params=params(8),
        cost_estimate=pl.CostEstimate(
            flops=count * m * depth, bytes_accessed=0, transcendentals=0
        ),
        name="down",
    )(table, *blocks, w_down, *more)


def down_last(table, total, first, second, slot, w_down, j, parts, experts, final):
    half, depth = first.shape
    m = 2 * half
    feats = w_down.shape[0]
    share = m // experts

    def kernel(tab, a_ref, b_ref, w_ref, total_ref, *refs):
        target = refs[-1] if final else refs[0]
        there = pl.ds(pl.multiple_of((tab[slot] * parts + j) * depth, depth), depth)
        target[:half, :] = total_ref[:half, :] + dot_nt(a_ref[...], w_ref[:, there])
        target[half:, :] = total_ref[half:, :] + dot_nt(b_ref[...], w_ref[:, there])
        if final:
            for i in range(experts):
                start = pl.multiple_of((tab[1] ^ i) * share, share)
                refs[i][...] = target[pl.ds(start, share), :].astype(jnp.bfloat16)

    if final:
        out_shape = [jax.ShapeDtypeStruct((share, feats), jnp.bfloat16)] * experts
        out_specs = [WHOLE] * experts
    else:
        out_shape = jax.ShapeDtypeStruct((m, feats), jnp.float32)
        out_specs = WHOLE
    return pl.pallas_call(
        kernel,
        grid_spec=pltpu.PrefetchScalarGridSpec(
            num_scalar_prefetch=1,
            in_specs=[WHOLE] * 4,
            out_specs=out_specs,
            scratch_shapes=[pltpu.VMEM((m, feats), jnp.float32)] if final else [],
        ),
        out_shape=out_shape,
        compiler_params=params(8),
        cost_estimate=pl.CostEstimate(
            flops=m * depth, bytes_accessed=0, transcendentals=0
        ),
        name="down_last",
    )(table, first, second, w_down, total)


def combine(table, pieces, order, routing, n, base):
    experts = len(pieces)
    share, feats = pieces[0].shape
    rows = routing.shape[0] // n
    group = share // rows

    def kernel(tab, *refs):
        ins, route_ref, outs, route = refs[:experts], refs[experts], refs[experts + 1 : -1], refs[-1]
        route[...] = route_ref[...].astype(jnp.float32)
        for k in range(group):
            block = lax.rem(k + tab[2], group)
            info = route[pl.ds(pl.multiple_of(tab[base + k] * rows, rows), rows), :]
            unit0 = info[:, 2:3] * 256.0 + info[:, 4:5]
            unit1 = info[:, 3:4] * 256.0 + info[:, 5:6]
            whole = unit0 + unit1
            share0, share1 = unit0 / whole, unit1 / whole
            mixed = jnp.zeros((rows, feats), jnp.float32)
            for spot, i in enumerate(order):
                name = (tab[1] ^ i).astype(jnp.float32)
                weight = jnp.where(info[:, 0:1] == name, share0, 0.0)
                weight += jnp.where(info[:, 1:2] == name, share1, 0.0)
                mixed += weight * ins[spot][block].astype(jnp.float32)
            outs[k][...] = mixed.astype(jnp.bfloat16)

    return pl.pallas_call(
        kernel,
        grid_spec=pltpu.PrefetchScalarGridSpec(
            num_scalar_prefetch=1,
            in_specs=[WHOLE] * (experts + 1),
            out_specs=[WHOLE] * group,
            scratch_shapes=[pltpu.VMEM(routing.shape, jnp.float32)],
        ),
        out_shape=[jax.ShapeDtypeStruct((rows, feats), jnp.bfloat16)] * group,
        compiler_params=params(16),
        name="combine",
    )(table, *[piece.reshape(group, rows, feats) for piece in pieces], routing)


def local(tokens, expert_ids, gate_units, gate_weight, up_weight, down_weight):
    experts = lax.axis_size("expert")
    n = lax.axis_size("tensor")
    group = n // experts
    rows, width = tokens.shape
    w_gate, w_up = (
        pltpu.with_memory_space_constraint(w[0], pltpu.HBM) for w in (gate_weight, up_weight)
    )
    w_down = down_weight[0]
    part = width // 2
    parts = 2 if w_gate.shape[1] % (2 * LANES) == 0 else 1

    me = lax.axis_index(("expert", "tensor")).astype(jnp.uint32)
    rows_of = jnp.asarray(tables(experts, n))
    length = rows_of.shape[1]
    table = lax.dynamic_slice(rows_of, (me, jnp.uint32(0)), (1, length)).reshape(length)

    ring = ring_of(n)
    ahead = [(ring[p], ring[(p + 1) % n]) for p in range(n)]
    behind = [(b, a) for a, b in ahead]

    core = (lax.axis_index("expert") & 1).reshape(1)
    own = prepare(core, tokens, expert_ids.T, gate_units.T)
    wanted = [(other, w) for other in (False, True) for w in (w_gate, w_up)]
    fetched = []

    def fetch_next(after):
        other, w = wanted[len(fetched)]

        def place(tab):
            return (1 - tab[0] if other else tab[0]) * part, slice(None)

        fetched.append(fetch(table, w, (part, w.shape[1]), place, after))

    brought = [own]
    forward = backward = own
    cut = part // 2
    for hop in range(1, n // 2 + 1):
        if hop > 1 and len(fetched) < len(wanted) + 1:
            forward, backward, fetched[-1] = lax.optimization_barrier(
                (forward, backward, fetched[-1])
            )
        if len(fetched) < len(wanted):
            fetch_next(forward)
        if hop < n // 2:
            forward = lax.ppermute(forward, "tensor", ahead)
            backward = lax.ppermute(backward, "tensor", behind)
            brought += [forward, backward]
        else:
            first = lax.ppermute(forward[:, :cut], "tensor", ahead)
            second = lax.ppermute(backward[:, cut:], "tensor", behind)
    while len(fetched) < len(wanted):
        fetch_next(forward)

    first, second, fetched[-1] = lax.optimization_barrier((first, second, fetched[-1]))
    far = jnp.concatenate([first, second], axis=1)
    collected, other = [], []
    for cols in (slice(0, cut), slice(cut, part), slice(part, part + LANES)):
        whole = jnp.zeros((n * rows, cols.stop - cols.start), tokens.dtype)
        for slot, block in enumerate(brought + [far]):
            whole = lax.dynamic_update_slice(whole, block[:, cols], (slot * rows, 0))
        collected.append(whole)
    gate_own, up_own, gate_other, up_other = fetched
    routing = collected[2]
    for q in range(2):
        other.append(lax.ppermute(collected[q], "expert", [(i, i ^ 1) for i in range(experts)]))
    sums = []
    for q in range(2):
        sums = depth_part(collected[q], gate_own, up_own, q, sums)
    sums = depth_part(other[0], gate_other, up_other, 0, sums)

    hidden = [
        hidden_part(table, other[1], gate_other, up_other, 1, sums, n, j, parts)
        for j in range(parts)
    ]
    total = None
    held = [([block], [3]) for block in hidden]
    half = n * rows // 2
    for hop in range(1, n // 2 + 1):
        came = []
        for j in range(parts):
            blocks, slots = held[j]
            if total is not None and hop > 1:
                blocks, total = lax.optimization_barrier((blocks, total))
            forward, backward = blocks[0], blocks[-1]
            if hop < n // 2:
                forward = lax.ppermute(forward, "tensor", ahead)
                backward = lax.ppermute(backward, "tensor", behind)
                held[j] = ([forward, backward], [2 + 2 * hop, 3 + 2 * hop])
            else:
                forward = lax.ppermute(forward[:half], "tensor", ahead)
                backward = lax.ppermute(backward[half:], "tensor", behind)
                held[j] = (forward, backward)
            came.append((blocks, [(slot, j) for slot in slots]))
            if hop > 1 and (hop < n // 2 or j < parts - 1):
                total = down_step(table, total, *came.pop(), w_down, parts)
        if hop == 1:
            own = lax.optimization_barrier([blocks for blocks, _ in came])
            for blocks, (_, places) in zip(own, came):
                total = down_step(table, total, blocks, places, w_down, parts)
    for j in range(parts):
        if j == parts - 1:
            total = down_step(table, total, *came.pop(), w_down, parts)
        total = down_last(
            table, total, *held[j], 2 + n, w_down, j, parts, experts, j == parts - 1
        )

    order = sorted(range(experts), key=lambda i: (i == 1, i & 1, i))
    pieces = [
        lax.ppermute(total[i], "expert", [(s, s ^ i) for s in range(experts)]) if i else total[0]
        for i in order
    ]
    mixed = combine(table, pieces, order, routing, n, 3 + n)
    arrived = []
    for k in range(group):
        pairs = []
        for e in range(experts):
            for t in range(n):
                pairs.append((e * n + t, (t // group) * n + group * e + (k + t) % group))
        arrived.append(lax.ppermute(mixed[k], ("expert", "tensor"), pairs))
    own = lax.axis_index("tensor") & (group - 1)
    spots = [(own - s) & (group - 1) for s in range(group)]
    return jnp.concatenate([lax.select_n(spot, *arrived) for spot in spots], axis=1)


def solution(mesh):
    return jax.shard_map(
        local,
        mesh=mesh,
        in_specs=(
            P("tensor", None),
            P("tensor", None),
            P("tensor", None),
            P("expert", None, "tensor"),
            P("expert", None, "tensor"),
            P("expert", "tensor", None),
        ),
        out_specs=P("tensor", "expert"),
        check_vma=False,
    )
```

```python
import jax
import jax.numpy as jnp
import numpy as np
from jax import lax
from jax.experimental import pallas as pl
from jax.experimental.pallas import tpu as pltpu
from jax.sharding import PartitionSpec as P

LANES = 128
WHOLE = pl.BlockSpec(memory_space=pltpu.VMEM)


def ring_of(count):
    return list(range(0, count, 2)) + list(range(count - 1, 0, -2))


def hop_list(count):
    hops = [0]
    for hop in range(1, count // 2):
        hops += [hop, -hop]
    return hops + [count // 2]


def tables(experts, n):
    ring = ring_of(n)
    hops = hop_list(n)
    group = n // experts
    rows = []
    for e in range(experts):
        for t in range(n):
            place = ring.index(t)
            sources = [ring[(place - hop) % n] for hop in hops]
            mine = [sources.index(group * e + (i + t) % group) for i in range(group)]
            rows.append([e % 2, e, t % group] + sources + mine)
    return np.array(rows, np.int32)


def params(megabytes):
    return pltpu.CompilerParams(vmem_limit_bytes=megabytes << 20)


def dot(a, b):
    return jnp.dot(a, b, preferred_element_type=jnp.float32)


def dot_nt(a, b):
    return lax.dot_general(a, b, (((1,), (1,)), ((), ())), preferred_element_type=jnp.float32)


def prepare(core, tokens, expert_ids, gate_units):
    rows, width = tokens.shape
    part = width // 2

    def kernel(core_ref, tokens_ref, ids_ref, units_ref, out, ids, units, sems):
        start = pl.multiple_of(core_ref[0] * part, part)
        copies = [
            pltpu.make_async_copy(source, target, sems.at[i])
            for i, (source, target) in enumerate(
                [
                    (ids_ref, ids),
                    (units_ref, units),
                    (tokens_ref.at[:, pl.ds(start, part)], out.at[:, :part]),
                ]
            )
        ]
        for copy in copies:
            copy.start()
        copies[0].wait()
        copies[1].wait()
        number = units[...]
        lines = [ids[...], number >> 8, number & 255]
        route = jnp.concatenate(
            [line.astype(jnp.float32) for line in lines] + [jnp.zeros((2, rows), jnp.float32)], axis=0
        )
        route = jnp.concatenate([route, jnp.zeros((8, LANES - rows), jnp.float32)], axis=1)
        route = jnp.concatenate([route, jnp.zeros((LANES - 8, LANES), jnp.float32)], axis=0)
        out[:, part:] = route.T[:rows, :].astype(jnp.bfloat16)
        copies[2].wait()

    hbm = pl.BlockSpec(memory_space=pltpu.HBM)
    return pl.pallas_call(
        kernel,
        grid_spec=pltpu.PrefetchScalarGridSpec(
            num_scalar_prefetch=1,
            in_specs=[hbm] * 3,
            out_specs=WHOLE,
            scratch_shapes=[
                pltpu.VMEM((2, rows), jnp.int32),
                pltpu.VMEM((2, rows), jnp.int32),
                pltpu.SemaphoreType.DMA((3,)),
            ],
        ),
        out_shape=pltpu.VMEM((rows, part + LANES), tokens.dtype),
        compiler_params=params(4),
        name="prepare",
    )(core, *[pltpu.with_memory_space_constraint(a, pltpu.HBM) for a in (tokens, expert_ids, gate_units)])


def bring(w_ref, out, sems, rows, columns):
    pieces = sems.shape[0]
    step = out.shape[0] // pieces
    copies = []
    for i in range(pieces):
        start = rows + i * step
        if not isinstance(start, int):
            start = pl.multiple_of(start, step)
        copies.append(
            pltpu.make_async_copy(
                w_ref.at[pl.ds(start, step), columns], out.at[pl.ds(i * step, step), :], sems.at[i]
            )
        )
    for copy in copies:
        copy.start()
    for copy in copies:
        copy.wait()


def fetch(table, weight, shape, place, after):
    pieces = next(k for k in (2, 1) if shape[0] % (k * 16) == 0)

    def kernel(tab, w_ref, after_ref, out, sems):
        del after_ref
        bring(w_ref, out, sems, *place(tab))

    return pl.pallas_call(
        kernel,
        grid_spec=pltpu.PrefetchScalarGridSpec(
            num_scalar_prefetch=1,
            in_specs=[
                pl.BlockSpec(memory_space=pltpu.HBM),
                pl.BlockSpec(memory_space=pl.ANY),
            ],
            out_specs=WHOLE,
            scratch_shapes=[pltpu.SemaphoreType.DMA((pieces,))],
        ),
        out_shape=pltpu.VMEM(shape, weight.dtype),
        compiler_params=params(4),
        cost_estimate=pl.CostEstimate(
            flops=0, bytes_accessed=4 * shape[0] * shape[1], transcendentals=0
        ),
        name="fetch",
    )(table, weight, after)


def column_tiles(units):
    size = 256 if units % 256 == 0 else units
    return [slice(i, i + size) for i in range(0, units, size)]


def depth_part(x, w_gate, w_up, q, sums):
    m, depth = x.shape
    units = w_gate.shape[1]
    rows = slice(q * depth, (q + 1) * depth)

    def kernel(x_ref, g_ref, u_ref, *refs):
        gate, up = refs[-2:]
        for cols in column_tiles(units):
            for w_ref, out, before in ((g_ref, gate, 0), (u_ref, up, 1)):
                product = dot(x_ref[...], w_ref[rows, cols])
                if sums:
                    product += refs[before][:, cols]
                out[:, cols] = product

    out = jax.ShapeDtypeStruct((m, units), jnp.float32)
    return pl.pallas_call(
        kernel,
        in_specs=[WHOLE] * (3 + len(sums)),
        out_specs=[WHOLE, WHOLE],
        out_shape=[out, out],
        compiler_params=params(8),
        cost_estimate=pl.CostEstimate(
            flops=4 * m * depth * units, bytes_accessed=4 * depth * units, transcendentals=0
        ),
        name="gate_up",
    )(x, w_gate, w_up, *sums)


def hidden_part(table, x, w_gate, w_up, q, sums, n, j, parts):
    m, depth = x.shape
    units = w_gate.shape[1] // parts
    rows = m // n
    deep = slice(q * depth, (q + 1) * depth)

    def kernel(tab, x_ref, g_ref, u_ref, gate_ref, up_ref, out):
        for cols in column_tiles(units):
            there = slice(j * units + cols.start, j * units + cols.stop)
            gate = gate_ref[:, there] + dot(x_ref[...], g_ref[deep, there])
            up = up_ref[:, there] + dot(x_ref[...], u_ref[deep, there])
            hidden = (gate * jax.nn.sigmoid(gate) * up).astype(out.dtype)
            for r in range(n):
                out[tab[3 + r], :, cols] = hidden[r * rows : (r + 1) * rows, :]

    return pl.pallas_call(
        kernel,
        grid_spec=pltpu.PrefetchScalarGridSpec(
            num_scalar_prefetch=1, in_specs=[WHOLE] * 5, out_specs=WHOLE
        ),
        out_shape=jax.ShapeDtypeStruct((n, rows, units), jnp.bfloat16),
        compiler_params=params(12),
        cost_estimate=pl.CostEstimate(
            flops=4 * m * depth * units, bytes_accessed=4 * depth * units, transcendentals=m * units
        ),
        name="hidden",
    )(table, x, w_gate, w_up, *sums).reshape(m, units)


def down_step(table, total, blocks, places, w_down, parts):
    m, depth = blocks[0].shape
    feats = w_down.shape[0]
    count = len(blocks)

    def kernel(tab, *refs):
        lhs, w_ref, out = refs[:count], refs[count], refs[-1]
        for i, (slot, j) in enumerate(places):
            start = pl.multiple_of((tab[slot] * parts + j) * depth, depth)
            product = dot_nt(lhs[i][...], w_ref[:, pl.ds(start, depth)])
            if i:
                out[...] += product
            elif total is None:
                out[...] = product
            else:
                out[...] = refs[count + 1][...] + product

    more = [] if total is None else [total]
    return pl.pallas_call(
        kernel,
        grid_spec=pltpu.PrefetchScalarGridSpec(
            num_scalar_prefetch=1,
            in_specs=[WHOLE] * (count + 1 + len(more)),
            out_specs=WHOLE,
        ),
        out_shape=jax.ShapeDtypeStruct((m, feats), jnp.float32),
        compiler_params=params(8),
        cost_estimate=pl.CostEstimate(
            flops=count * m * depth, bytes_accessed=0, transcendentals=0
        ),
        name="down",
    )(table, *blocks, w_down, *more)


def down_last(table, total, first, second, slot, w_down, j, parts, experts, final):
    half, depth = first.shape
    m = 2 * half
    feats = w_down.shape[0]
    share = m // experts

    def kernel(tab, a_ref, b_ref, w_ref, total_ref, *refs):
        target = refs[-1] if final else refs[0]
        there = pl.ds(pl.multiple_of((tab[slot] * parts + j) * depth, depth), depth)
        target[:half, :] = total_ref[:half, :] + dot_nt(a_ref[...], w_ref[:, there])
        target[half:, :] = total_ref[half:, :] + dot_nt(b_ref[...], w_ref[:, there])
        if final:
            for i in range(experts):
                start = pl.multiple_of((tab[1] ^ i) * share, share)
                refs[i][...] = target[pl.ds(start, share), :].astype(jnp.bfloat16)

    if final:
        out_shape = [jax.ShapeDtypeStruct((share, feats), jnp.bfloat16)] * experts
        out_specs = [WHOLE] * experts
    else:
        out_shape = jax.ShapeDtypeStruct((m, feats), jnp.float32)
        out_specs = WHOLE
    return pl.pallas_call(
        kernel,
        grid_spec=pltpu.PrefetchScalarGridSpec(
            num_scalar_prefetch=1,
            in_specs=[WHOLE] * 4,
            out_specs=out_specs,
            scratch_shapes=[pltpu.VMEM((m, feats), jnp.float32)] if final else [],
        ),
        out_shape=out_shape,
        compiler_params=params(8),
        cost_estimate=pl.CostEstimate(
            flops=m * depth, bytes_accessed=0, transcendentals=0
        ),
        name="down_last",
    )(table, first, second, w_down, total)


def combine(table, pieces, order, routing, n, base):
    experts = len(pieces)
    share, feats = pieces[0].shape
    rows = routing.shape[0] // n
    group = share // rows

    def kernel(tab, *refs):
        ins, route_ref, outs, route = refs[:experts], refs[experts], refs[experts + 1 : -1], refs[-1]
        route[...] = route_ref[...].astype(jnp.float32)
        for k in range(group):
            block = lax.rem(k + tab[2], group)
            info = route[pl.ds(pl.multiple_of(tab[base + k] * rows, rows), rows), :]
            unit0 = info[:, 2:3] * 256.0 + info[:, 4:5]
            unit1 = info[:, 3:4] * 256.0 + info[:, 5:6]
            whole = unit0 + unit1
            share0, share1 = unit0 / whole, unit1 / whole
            mixed = jnp.zeros((rows, feats), jnp.float32)
            for spot, i in enumerate(order):
                name = (tab[1] ^ i).astype(jnp.float32)
                weight = jnp.where(info[:, 0:1] == name, share0, 0.0)
                weight += jnp.where(info[:, 1:2] == name, share1, 0.0)
                mixed += weight * ins[spot][block].astype(jnp.float32)
            outs[k][...] = mixed.astype(jnp.bfloat16)

    return pl.pallas_call(
        kernel,
        grid_spec=pltpu.PrefetchScalarGridSpec(
            num_scalar_prefetch=1,
            in_specs=[WHOLE] * (experts + 1),
            out_specs=[WHOLE] * group,
            scratch_shapes=[pltpu.VMEM(routing.shape, jnp.float32)],
        ),
        out_shape=[jax.ShapeDtypeStruct((rows, feats), jnp.bfloat16)] * group,
        compiler_params=params(16),
        name="combine",
    )(table, *[piece.reshape(group, rows, feats) for piece in pieces], routing)


def local(tokens, expert_ids, gate_units, gate_weight, up_weight, down_weight):
    experts = lax.axis_size("expert")
    n = lax.axis_size("tensor")
    group = n // experts
    rows, width = tokens.shape
    w_gate, w_up = (
        pltpu.with_memory_space_constraint(w[0], pltpu.HBM) for w in (gate_weight, up_weight)
    )
    w_down = down_weight[0]
    part = width // 2
    parts = 2 if w_gate.shape[1] % (2 * LANES) == 0 else 1

    me = lax.axis_index(("expert", "tensor")).astype(jnp.uint32)
    rows_of = jnp.asarray(tables(experts, n))
    length = rows_of.shape[1]
    table = lax.dynamic_slice(rows_of, (me, jnp.uint32(0)), (1, length)).reshape(length)

    ring = ring_of(n)
    ahead = [(ring[p], ring[(p + 1) % n]) for p in range(n)]
    behind = [(b, a) for a, b in ahead]

    core = (lax.axis_index("expert") & 1).reshape(1)
    own = prepare(core, tokens, expert_ids.T, gate_units.T)
    wanted = [(other, w) for other in (False, True) for w in (w_gate, w_up)]
    fetched = []

    def fetch_next(after):
        other, w = wanted[len(fetched)]

        def place(tab):
            return (1 - tab[0] if other else tab[0]) * part, slice(None)

        fetched.append(fetch(table, w, (part, w.shape[1]), place, after))

    brought = [own]
    forward = backward = own
    cut = part // 2
    for hop in range(1, n // 2 + 1):
        if hop > 1 and len(fetched) < len(wanted) + 1:
            forward, backward, fetched[-1] = lax.optimization_barrier(
                (forward, backward, fetched[-1])
            )
        if len(fetched) < len(wanted):
            fetch_next(forward)
        if hop < n // 2:
            forward = lax.ppermute(forward, "tensor", ahead)
            backward = lax.ppermute(backward, "tensor", behind)
            brought += [forward, backward]
        else:
            first = lax.ppermute(forward[:, :cut], "tensor", ahead)
            second = lax.ppermute(backward[:, cut:], "tensor", behind)
    while len(fetched) < len(wanted):
        fetch_next(forward)

    first, second, fetched[-1] = lax.optimization_barrier((first, second, fetched[-1]))
    far = jnp.concatenate([first, second], axis=1)
    collected, other = [], []
    for cols in (slice(0, cut), slice(cut, part), slice(part, part + LANES)):
        whole = jnp.zeros((n * rows, cols.stop - cols.start), tokens.dtype)
        for slot, block in enumerate(brought + [far]):
            whole = lax.dynamic_update_slice(whole, block[:, cols], (slot * rows, 0))
        collected.append(whole)
    gate_own, up_own, gate_other, up_other = fetched
    routing = collected[2]
    for q in range(2):
        other.append(lax.ppermute(collected[q], "expert", [(i, i ^ 1) for i in range(experts)]))
    sums = []
    for q in range(2):
        sums = depth_part(collected[q], gate_own, up_own, q, sums)
    sums = depth_part(other[0], gate_other, up_other, 0, sums)

    hidden = [
        hidden_part(table, other[1], gate_other, up_other, 1, sums, n, j, parts)
        for j in range(parts)
    ]
    total = None
    held = [([block], [3]) for block in hidden]
    half = n * rows // 2
    for hop in range(1, n // 2 + 1):
        came = []
        for j in range(parts):
            blocks, slots = held[j]
            if total is not None and hop > 1:
                blocks, total = lax.optimization_barrier((blocks, total))
            forward, backward = blocks[0], blocks[-1]
            if hop < n // 2:
                forward = lax.ppermute(forward, "tensor", ahead)
                backward = lax.ppermute(backward, "tensor", behind)
                held[j] = ([forward, backward], [2 + 2 * hop, 3 + 2 * hop])
            else:
                forward = lax.ppermute(forward[:half], "tensor", ahead)
                backward = lax.ppermute(backward[half:], "tensor", behind)
                held[j] = (forward, backward)
            came.append((blocks, [(slot, j) for slot in slots]))
            if hop > 1 and (hop < n // 2 or j < parts - 1):
                total = down_step(table, total, *came.pop(), w_down, parts)
        if hop == 1:
            own = lax.optimization_barrier([blocks for blocks, _ in came])
            for blocks, (_, places) in zip(own, came):
                total = down_step(table, total, blocks, places, w_down, parts)
    for j in range(parts):
        if j == parts - 1:
            total = down_step(table, total, *came.pop(), w_down, parts)
        total = down_last(
            table, total, *held[j], 2 + n, w_down, j, parts, experts, j == parts - 1
        )

    order = sorted(range(experts), key=lambda i: (i == 1, i & 1, i))
    pieces = [
        lax.ppermute(total[i], "expert", [(s, s ^ i) for s in range(experts)]) if i else total[0]
        for i in order
    ]
    mixed = combine(table, pieces, order, routing, n, 3 + n)
    arrived = []
    for k in range(group):
        pairs = []
        for e in range(experts):
            for t in range(n):
                pairs.append((e * n + t, (t // group) * n + group * e + (k + t) % group))
        arrived.append(lax.ppermute(mixed[k], ("expert", "tensor"), pairs))
    own = lax.axis_index("tensor") & (group - 1)
    spots = [(own - s) & (group - 1) for s in range(group)]
    return jnp.concatenate([lax.select_n(spot, *arrived) for spot in spots], axis=1)


def solution(mesh):
    return jax.shard_map(
        local,
        mesh=mesh,
        in_specs=(
            P("tensor", None),
            P("tensor", None),
            P("tensor", None),
            P("expert", None, "tensor"),
            P("expert", None, "tensor"),
            P("expert", "tensor", None),
        ),
        out_specs=P("tensor", "expert"),
        check_vma=False,
    )
```
